128 devices in a mesh: rve: 4 (over x), slab: 32 (over z, y, core).
Axes of the slice: x: 4, y: 4, z: 4, core: 2. Of those that a mesh axis runs over, the one named last changes fastest.
Arguments:
- plastic_strain: float32 [6, 4, 96, 9216], P(None, 'rve', 'slab'), may hold values from -2 to 2
- hardening_var: float32 [4, 96, 9216], P('rve', 'slab'), may hold values from 0 to 1
- strain_start: float32 [6, 4, 96, 9216], P(None, 'rve', 'slab'), may hold values from -6 to 6
- strain_step: float32 [6, 4, 96, 9216], P(None, 'rve', 'slab'), may hold values from -4 to 4
- shear_mod: float32 [4, 96, 9216], P('rve', 'slab'), may hold values from 0.5 to 2
- bulk_mod: float32 [4, 96, 9216], P('rve', 'slab'), may hold values from 1 to 4
- yield_stress: float32 [4, 96, 9216], P('rve', 'slab'), may hold values from 0.5 to 4
- substeps: int32 [4, 384], replicated, may hold values from 1 to 8, as said below
- pull_group: int32 [4, 64], replicated, may hold values from 0 to 3, as said below
- pull_block: int32 [4, 64], replicated, may hold values from 0 to 383, as said below
- owner: int32 [4], replicated, may hold values from 0 to 3
Outputs:
- correction: float32 [3, 4, 96, 9216], P(None, 'rve', 'slab')
- inbox: float32 [7, 4, 64, 2304], P(None, 'rve', 'slab')
- element_sums: float32 [4, 42], P('rve')
The draws below stay inside these ranges and needn't reach their ends.
Inputs may be any that keep to these rules, and one draw needn't show every extreme that they name: `substeps`: every RVE has a block with exactly its largest count, and some RVE reaches 8. `pull_group`: for each group g and each slab s, the 2 slots k with k // 2 = s name distinct source groups. `pull_block`: slot k names a block of z-slab k // 2: an id from (k // 2) * 4 * 3 to (k // 2 + 1) * 4 * 3 - 1.
All inputs are finite; a program needn't handle non-finite values.
Results may differ from the reference program's by a relative error of at most 0.0003.
Values sent between devices are 32-bit elements; how exact they have to be, the bound alone decides.
No kernel may reach another device: no remote copies, remote signals or barrier semaphores. Data moves between devices by JAX's collectives and lax.ppermute only.
A program may use at most 128 MiB of HBM per device.

```python
import math
import jax
import jax.numpy as jnp
from jax import lax

NVX = 96
NZ = 96
ITERS = 5
SUBMAX = 8
SZ = 3
PLANE = 9216
BLK = 2304
NBLK = 384
RVES = 4
IN_DEV = 2
INBOX = 64


def pull_plan(key):
    slab_total = INBOX // IN_DEV
    key_list = jax.random.split(jax.random.fold_in(key, 11), RVES * slab_total)

    def choose(single):
        return jax.random.permutation(single, RVES)[:IN_DEV]
    sources = jax.vmap(choose)(key_list).reshape(RVES, INBOX)
    offsets = jax.random.randint(jax.random.fold_in(key, 12), (RVES, INBOX), 0, 4 * SZ)
    slots = jnp.arange(INBOX)
    blocks = (slots // IN_DEV)[None, :] * (4 * SZ) + offsets
    return (sources.astype(jnp.int32), blocks.astype(jnp.int32))


def draw_pull_group(key, part):
    return pull_plan(key)[0]


def draw_pull_block(key, part):
    return pull_plan(key)[1]


def draw_substeps(key, part):
    level = jax.random.randint(jax.random.fold_in(key, 21), (RVES,), 1, SUBMAX + 1)
    forced = jax.random.randint(jax.random.fold_in(key, 22), (), 0, RVES)
    level = jnp.where(jnp.arange(RVES) == forced, SUBMAX, level)
    raw = jax.random.randint(jax.random.fold_in(key, 23), (RVES, NBLK), 0, 1000000) % level[:, None] + 1
    special = jax.random.randint(jax.random.fold_in(key, 24), (RVES,), 0, NBLK)
    costs = jnp.where(jnp.arange(NBLK)[None, :] == special[:, None], level[:, None], raw)
    return costs.astype(jnp.int32)


def with_ends(values, rng, low, largest):
    extent = values.shape
    index_at = [jax.random.randint(jax.random.fold_in(rng, axis), (), 0, extent[axis]) for axis in range(len(extent))]
    values = values.at[tuple(index_at)].set(low)
    longest = extent.index(max(extent))
    index_at[longest] = (index_at[longest] + 1) % extent[longest]
    return values.at[tuple(index_at)].set(largest)


def block_levels(stream_key, extent, cuts, low, high):
    loudness = 1.0
    for position, shards_of in cuts:
        draws = jax.random.uniform(jax.random.fold_in(jax.random.fold_in(stream_key, 6), position), (shards_of,), jnp.float32, low / len(cuts), high / len(cuts))
        loudness = loudness * jnp.repeat(jnp.exp(draws), extent[position] // shards_of).reshape((-1,) + (1,) * (len(extent) - 1 - position))
    return loudness


def bell_draw(key, shape, deviation, most, shards=(), kind=jnp.bfloat16):
    result = deviation * jax.random.normal(key, shape, jnp.float32)
    if shards:
        result = result * block_levels(key, shape, shards, -0.22, 0.18)
    return jnp.clip(result, -most, most).astype(kind)


def setup_inputs(seed: int = 0) -> dict:
    splits = jax.random.split(jax.random.key(seed), 12)
    plastic_strain = bell_draw(splits[0], (6, RVES, NZ, PLANE), 0.3, 2.0, ((1, 4), (2, 32)), jnp.float32)
    hardening_var = jnp.clip(1.0 * jax.random.uniform(splits[1], (RVES, NZ, PLANE), jnp.float32) ** block_levels(splits[1], (RVES, NZ, PLANE), ((0, 4), (1, 32)), -0.2, 0.2), 0.0, 1.0)
    strain_start = bell_draw(splits[2], (6, RVES, NZ, PLANE), 1.0, 6.0, ((1, 4), (2, 32)), jnp.float32)
    strain_step = bell_draw(splits[3], (6, RVES, NZ, PLANE), 0.5, 4.0, ((1, 4), (2, 32)), jnp.float32)
    shear_mod = jnp.clip(jnp.exp(math.log(2.0) - 1.3862944 * jax.random.uniform(splits[4], (RVES, NZ, PLANE), jnp.float32) ** block_levels(splits[4], (RVES, NZ, PLANE), ((0, 4), (1, 32)), -0.2, 0.2)), 0.5, 2.0)
    bulk_mod = jnp.clip(jnp.exp(math.log(4.0) - 1.3862944 * jax.random.uniform(splits[5], (RVES, NZ, PLANE), jnp.float32) ** block_levels(splits[5], (RVES, NZ, PLANE), ((0, 4), (1, 32)), -0.2, 0.2)), 1.0, 4.0)
    yield_stress = jnp.clip(jnp.exp(math.log(4.0) - 2.0794415 * jax.random.uniform(splits[6], (RVES, NZ, PLANE), jnp.float32) ** block_levels(splits[6], (RVES, NZ, PLANE), ((0, 4), (1, 32)), -0.2, 0.2)), 0.5, 4.0)
    substeps = draw_substeps(jax.random.fold_in(splits[11], 71), 0)
    pull_group = draw_pull_group(jax.random.fold_in(splits[11], 71), 0)
    pull_block = draw_pull_block(jax.random.fold_in(splits[11], 71), 0)
    owner = with_ends(jax.random.randint(splits[10], (RVES,), 0, RVES), jax.random.fold_in(splits[10], 1), 0, RVES - 1).astype(jnp.int32)
    return {"plastic_strain": plastic_strain, "hardening_var": hardening_var, "strain_start": strain_start, "strain_step": strain_step, "shear_mod": shear_mod, "bulk_mod": bulk_mod, "yield_stress": yield_stress, "substeps": substeps, "pull_group": pull_group, "pull_block": pull_block, "owner": owner}


hard_ratio = 0.3
mass_weight = 0.05
root_two_thirds = math.sqrt(2.0 / 3.0)
half_root = 1.0 / math.sqrt(2.0)

def stencil_offsets():
    listing = []
    for depth_step in (-1, 0, 1):
        for row_step in (-1, 0, 1):
            for column_step in (-1, 0, 1):
                reach = abs(depth_step) + abs(row_step) + abs(column_step)
                if reach > 0:
                    listing.append((depth_step, row_step, column_step, (1.0, 0.5, 0.25)[reach - 1]))
    return listing

def plane_shift(values, row_step, column_step):
    if row_step != 0:
        values = jnp.roll(values, -row_step * NVX, axis=-1)
    if column_step != 0:
        column = jnp.arange(PLANE) % NVX
        plain = jnp.roll(values, -column_step, axis=-1)
        wrapped = jnp.roll(values, column_step * NVX - column_step, axis=-1)
        border = NVX - 1 if column_step > 0 else 0
        values = jnp.where(column == border, wrapped, plain)
    return values

def trace_vector(ndim):
    return jnp.array([1.0, 1.0, 1.0, 0.0, 0.0, 0.0], jnp.float32).reshape((6,) + (1,) * (ndim - 1))

def deviator_of(strain, plastic):
    elastic = strain - plastic
    volume = elastic[0] + elastic[1] + elastic[2]
    return (elastic - volume / 3.0 * trace_vector(strain.ndim), volume)

def return_map(plastic, hardening, strain_begin, strain_delta, shear_field, bulk_field, yield_field, count, turns):
    harden = hard_ratio * shear_field

    def substep(turn, carry):
        plastic_now, hardening_now, increment, direction, floored = carry
        turn_float = jnp.asarray(turn).astype(jnp.float32)
        strain = strain_begin + (turn_float + 1.0) / count * strain_delta
        deviator, volume = deviator_of(strain, plastic_now)
        trial = 2.0 * shear_field * deviator
        magnitude = jnp.sqrt(lax.optimization_barrier(jnp.sum(trial * trial, axis=0)))
        excess = magnitude - root_two_thirds * (yield_field + harden * hardening_now)
        active = turn_float < count
        new_increment = jnp.maximum(excess, 0.0) / (2.0 * shear_field + 2.0 / 3.0 * harden)
        new_floored = jnp.maximum(magnitude, root_two_thirds * yield_field)
        new_direction = trial / new_floored
        new_increment = jnp.where(active, new_increment, 0.0)
        plastic_now = plastic_now + new_increment * new_direction
        hardening_now = hardening_now + root_two_thirds * new_increment
        increment = jnp.where(active, new_increment, increment)
        direction = jnp.where(active, new_direction, direction)
        floored = jnp.where(active, new_floored, floored)
        return (plastic_now, hardening_now, increment, direction, floored)
    start = (plastic, hardening, jnp.zeros_like(hardening), jnp.zeros_like(plastic), jnp.ones_like(hardening))
    plastic_new, hardening_new, increment, direction, floored = lax.fori_loop(0, turns, substep, start)
    deviator, volume = deviator_of(strain_begin + strain_delta, plastic_new)
    stress = bulk_field * volume * trace_vector(plastic.ndim) + 2.0 * shear_field * deviator
    theta = 1.0 - 2.0 * shear_field * increment / floored
    coefficient = shear_field * theta
    weight = shear_field * (theta - 1.0)
    return (stress, coefficient, plastic_new, hardening_new, weight, direction)

def rhs_from(stress, depth_diff):
    row_diff = 0.5 * (plane_shift(stress, 1, 0) - plane_shift(stress, -1, 0))
    column_diff = 0.5 * (plane_shift(stress, 0, 1) - plane_shift(stress, 0, -1))
    return jnp.stack([column_diff[0] + half_root * (row_diff[5] + depth_diff[4]), half_root * (column_diff[5] + depth_diff[3]) + row_diff[1], half_root * (column_diff[4] + row_diff[3]) + depth_diff[2]])

def apply_operator(field, coefficient):
    total = mass_weight * coefficient * field
    for depth_step, row_step, column_step, weight in stencil_offsets():
        other = plane_shift(jnp.roll(field, -depth_step, axis=-2), row_step, column_step)
        other_coef = plane_shift(jnp.roll(coefficient, -depth_step, axis=-2), row_step, column_step)
        total = total + 0.5 * weight * (coefficient + other_coef) * (field - other)
    return total

def finish(sums):
    trace_vec = jnp.array([1.0, 1.0, 1.0, 0.0, 0.0, 0.0], jnp.float32)
    outer = trace_vec[:, None] * trace_vec[None, :]
    projector = jnp.eye(6, dtype=jnp.float32) - outer / 3.0
    tangent = sums[6] * outer + 2.0 * sums[7] * projector + 2.0 * sums[8:].reshape(6, 6)
    return jnp.concatenate([sums[:6], tangent.reshape(36)])

def one_rve(items):
    plastic, hardening, begin, delta, shear_field, bulk_field, yield_field, costs = items
    count = jnp.broadcast_to(costs.astype(jnp.float32)[:, None], (NBLK, BLK)).reshape(NZ, PLANE)
    stress, coefficient, plastic_new, hardening_new, weight, direction = return_map(plastic, hardening, begin, delta, shear_field, bulk_field, yield_field, count, SUBMAX)
    volume = float(NZ * PLANE)
    flat_direction = direction.reshape(6, NZ * PLANE)
    coupling = jnp.dot(weight.reshape(1, NZ * PLANE) * flat_direction, flat_direction.T, precision=lax.Precision.HIGHEST)
    sums = jnp.concatenate([lax.optimization_barrier(jnp.sum(stress, axis=(1, 2))), jnp.sum(bulk_field)[None], jnp.sum(coefficient)[None], coupling.reshape(36)]) / volume
    depth_diff = 0.5 * (jnp.roll(stress, -1, axis=-2) - jnp.roll(stress, 1, axis=-2))
    rhs = rhs_from(stress, depth_diff)
    solution = jnp.zeros_like(rhs)
    residual = rhs
    direction_cg = rhs
    norm_now = jnp.sum(residual * residual)
    for turn in range(ITERS):
        image = apply_operator(direction_cg, coefficient)
        alpha = norm_now / jnp.sum(direction_cg * image)
        solution = solution + alpha * direction_cg
        residual = residual - alpha * image
        norm_next = jnp.sum(residual * residual)
        direction_cg = residual + norm_next / norm_now * direction_cg
        norm_now = norm_next
    history = jnp.concatenate([plastic_new, hardening_new[None]], axis=0)
    return (solution, history, finish(sums))

def reference(plastic_strain, hardening_var, strain_start, strain_step, shear_mod, bulk_mod, yield_stress, substeps, pull_group, pull_block, owner):
    items = (jnp.moveaxis(plastic_strain, 1, 0), hardening_var, jnp.moveaxis(strain_start, 1, 0), jnp.moveaxis(strain_step, 1, 0), shear_mod, bulk_mod, yield_stress, substeps)
    solutions, histories, summaries = lax.map(one_rve, items)
    correction = jnp.moveaxis(solutions, 0, 1)
    blocks = histories.reshape(RVES, 7, NBLK, BLK)
    picked = blocks[pull_group, :, pull_block, :]
    inbox = jnp.transpose(picked, (2, 0, 1, 3))
    table = (owner[None, :] == jnp.arange(RVES)[:, None]).astype(jnp.float32)
    element_sums = jnp.dot(table, summaries, precision=lax.Precision.HIGHEST)
    return (correction, inbox, element_sums)
```

```python
import math

import jax
import jax.numpy as jnp
from jax import lax
from jax.experimental import pallas as pl
from jax.experimental.pallas import tpu as pltpu
from jax.sharding import PartitionSpec as P

NVX = 96
LANES = 128
FLAT = 72
DEPTH = 3
BLOCK_ROWS = 18
BLOCKS = 12
VOXELS = 884736.0
F32 = jnp.float32

root_two_thirds = math.sqrt(2.0 / 3.0)
half_root = 1.0 / math.sqrt(2.0)
RETURN = 2.0 / 2.2
HARDEN = 0.2 / 2.2

BULK_LANE = 42
COEF_LANE = 43
SUM_BASE = 64
PAIRS = [(i, j) for i in range(6) for j in range(i, 6) if (i, j) != (5, 5)]

UP_A = 11
UP_B = 19


def roll(values, shift, axis):
    return pltpu.roll(values, shift % values.shape[axis], axis)


def lane_of(rows):
    return lax.broadcasted_iota(jnp.int32, (rows, LANES), 1)


def widen(flat_ref, at, wide_ref, to):
    lane = lane_of(24)
    a0, a1, a2 = [flat_ref[(*at, pl.ds(i, 24, stride=3), slice(None))] for i in range(3)]
    r1 = roll(a1, 64, 1)
    rows = [
        a0,
        jnp.where(lane < 32, roll(a0, 32, 1), roll(a1, 32, 1)),
        jnp.where(lane < 64, r1, roll(a2, 64, 1)),
        roll(a2, 96, 1),
    ]
    for i, row in enumerate(rows):
        full = jnp.where(lane < 96, row, jnp.where(lane < 112, roll(row, 96, 1), roll(row, 32, 1)))
        wide_ref[(*to, pl.ds(i, 24, stride=4), slice(None))] = full


def narrow(wide_ref, at):
    lane = lane_of(24)
    o0, o1, o2, o3 = [wide_ref[(*at, pl.ds(i, 24, stride=4), slice(None))] for i in range(4)]
    r1, r2, r3 = roll(o1, 96, 1), roll(o2, 64, 1), roll(o3, 32, 1)
    return (
        jnp.where(lane < 96, o0, r1),
        jnp.where(lane < 64, r1, r2),
        jnp.where(lane < 32, r2, r3),
    )


def put(rows, *targets):
    for ref, to in targets:
        for i in range(3):
            ref[(*to, pl.ds(i, 24, stride=3), slice(None))] = rows[i]


def smooth_plane(values):
    values = values + roll(values, 1, 0)
    values = values + roll(values, -1, 0)
    values = values + roll(values, 1, 1)
    return values + roll(values, -1, 1)


def operator(u, e, d):
    once = (u[0] + u[2]) + (u[1] + u[1])
    mid = e[1] * u[1]
    twice = (e[0] * u[0] + e[2] * u[2]) + (mid + mid)
    return d * u[1] - e[1] * smooth_plane(once) - smooth_plane(twice)


def diagonal(e):
    return 64.4 * e[1] + smooth_plane((e[0] + e[2]) + (e[1] + e[1]))


def three(ref, *at):
    *lead, mid = at
    return [ref[(*lead, mid + k)] for k in (-1, 0, 1)]


def total(values):
    return jnp.sum(jnp.sum(values, axis=0, keepdims=True), axis=1, keepdims=True)


def fold(values):
    out = values[0:8]
    for i in range(8, values.shape[0], 8):
        out = out + values[i : i + 8]
    return out


def pick(row, lane, k):
    return jnp.sum(jnp.where(lane == k, row, 0.0), axis=1, keepdims=True)


def on_plane_loop(count, body):
    lax.fori_loop(0, count, lambda i, c: (body(i), c)[1], 0)


def map_kernel(
    ids,
    counts,
    plastic,
    hard,
    begin,
    delta,
    shear,
    bulk,
    yields,
    up,
    down,
    own,
    pull,
    e_wide,
    history,
    dev,
    extra,
    flat,
    wide,
):
    group, first = ids[0], ids[1] * BLOCKS
    row = lax.broadcasted_iota(jnp.int32, (FLAT, LANES), 0)

    def plane(z):
        block = [counts[group, first + 4 * z + b] for b in range(4)]
        turns = jnp.maximum(jnp.maximum(block[0], block[1]), jnp.maximum(block[2], block[3]))
        held = jnp.where(
            row < 2 * BLOCK_ROWS,
            jnp.where(row < BLOCK_ROWS, block[0], block[1]),
            jnp.where(row < 3 * BLOCK_ROWS, block[2], block[3]),
        )
        share = 1.0 / held.astype(F32)
        twice_mu = 2.0 * shear[z]
        elastic = [begin[i, z] - plastic[i, z] for i in range(6)]
        step = [delta[i, z] for i in range(6)]
        third0 = (elastic[0] + elastic[1] + elastic[2]) * (1.0 / 3.0)
        third1 = (step[0] + step[1] + step[2]) * (1.0 / 3.0)
        stress = [twice_mu * (elastic[i] - third0 if i < 3 else elastic[i]) for i in range(6)]
        rate = twice_mu * share
        for i in range(6):
            flat[i] = rate * (step[i] - third1 if i < 3 else step[i])
        floor = root_two_thirds * yields[z]
        limit0 = floor + (root_two_thirds * 0.15) * twice_mu * hard[z]
        most = 1.0 / floor

        def substep(t, carry):
            *s, gone, _, _ = carry
            act = jnp.where(held >= turns - t, 1.0, 0.0)
            s = [s[i] + act * flat[i] for i in range(6)]
            square = s[0] * s[0]
            for i in range(1, 6):
                square = square + s[i] * s[i]
            square = jnp.maximum(square, 1e-30)
            inverse = lax.rsqrt(square)
            over = jnp.maximum(square * inverse - (limit0 + HARDEN * gone), 0.0) * act
            inverse = jnp.minimum(inverse, most)
            theta = 1.0 - (RETURN * over) * inverse
            return (*[theta * s[i] for i in range(6)], gone + over, theta, inverse)

        zero = jnp.zeros((FLAT, LANES), F32)
        *s, gone, theta, inverse = lax.fori_loop(0, turns, substep, (*stress, zero, zero, zero))
        mu = 0.5 * twice_mu
        per = 1.0 / twice_mu
        elastic = [begin[i, z] - plastic[i, z] + delta[i, z] for i in range(6)]
        trace = elastic[0] + elastic[1] + elastic[2]
        third = trace * (1.0 / 3.0)
        for i in range(6):
            whole = elastic[i] - third if i < 3 else elastic[i]
            history[i, z] = plastic[i, z] + (whole - per * s[i])
            dev[i, z] = s[i]
        history[6, z] = hard[z] + (root_two_thirds / 1.1) * per * gone
        pressure = bulk[z] * trace
        ratio = inverse / theta
        coef = mu * theta
        extra[0, z] = pressure
        extra[1, z] = mu * (theta - 1.0) * (ratio * ratio)
        extra[2, z] = coef
        for i in range(6):
            flat[i] = pressure + s[i] if i < 3 else s[i]
        flat[6] = coef * (1.0 / 128.0)
        on_plane_loop(7, lambda i: widen(flat, (i,), wide, (i,)))
        e_wide[z] = wide[6]

        def along_x(u):
            return roll(u, -1, 1) - roll(u, 1, 1)

        def along_y(u):
            return roll(u, -1, 0) - roll(u, 1, 0)

        half = 0.5 * half_root
        own[0, z] = 0.5 * along_x(wide[0]) + half * along_y(wide[5])
        own[1, z] = half * along_x(wide[5]) + 0.5 * along_y(wide[1])
        own[2, z] = half * (along_x(wide[4]) + along_y(wide[3]))
        pull[0, z] = half * wide[4]
        pull[1, z] = half * wide[3]
        pull[2, z] = 0.5 * wide[2]

    on_plane_loop(DEPTH, plane)

    def finish(c):
        own[c, 0] = own[c, 0] + pull[c, 1]
        own[c, 1] = own[c, 1] + pull[c, 2] - pull[c, 0]
        own[c, 2] = own[c, 2] - pull[c, 1]
        put(narrow(own, (c, 1)), (up, (c,)), (down, (c,)))
        put(narrow(own, (c, 2)), (up, (3 + c,)))
        put(narrow(own, (c, 0)), (down, (3 + c,)))

    on_plane_loop(3, finish)
    half = 0.5 * half_root
    for ref, z in ((up, 2), (down, 0)):
        ref[6] = half * dev[4, z]
        ref[7] = half * dev[3, z]
        ref[8] = 0.5 * (dev[2, z] + extra[0, z])
        ref[9] = extra[2, 1] * (1.0 / 128.0)
        ref[10] = extra[2, z] * (1.0 / 128.0)


def sums_kernel(ids, pull_group, pull_block, dev, extra, bulk, history, send, kept):
    group, slab = ids[0], ids[1]
    lane = lane_of(1)
    pairs = [(i, j) for i in range(6) for j in range(i, 6)]

    def chunk(t, carry):
        z, at = t // 3, pl.multiple_of((t % 3) * 24, 8)
        rows = pl.ds(at, 24)
        s = [dev[i, z, rows] for i in range(6)]
        pressure = extra[0, z, rows]
        weighted = extra[1, z, rows]
        terms = [pressure + s[i] if i < 3 else s[i] for i in range(6)]
        terms += [bulk[z, rows], extra[2, z, rows]]
        ws = [weighted * v for v in s]
        terms += [ws[i] * s[j] for i, j in pairs]
        return tuple(c + fold(v) for c, v in zip(carry, terms))

    zero = jnp.zeros((8, LANES), F32)
    sums = lax.fori_loop(0, 9, chunk, (zero,) * (8 + len(pairs)))
    sums = [total(v) * (1.0 / VOXELS) for v in sums]
    row = jnp.zeros((1, LANES), F32)
    for i in range(6):
        row = jnp.where(lane == i, sums[i], row)
    row = jnp.where(lane == BULK_LANE, sums[6], row)
    row = jnp.where(lane == COEF_LANE, sums[7], row)
    for k, (i, j) in enumerate(pairs):
        hit = (lane == 6 + 6 * i + j) | (lane == 6 + 6 * j + i)
        row = jnp.where(hit, sums[8 + k], row)

    for shift in range(4):
        to = lax.rem(group + shift, 4)
        first = pull_group[to, 2 * slab] == group
        at = jnp.where(first, pull_block[to, 2 * slab], pull_block[to, 2 * slab + 1])
        at = jnp.clip(at - slab * BLOCKS, 0, BLOCKS - 1)
        z, part = at // 4, at % 4
        for b in range(4):

            @pl.when(part == b)
            def _():
                for i in range(7):
                    block = history[i, z, pl.ds(BLOCK_ROWS * b, BLOCK_ROWS)]
                    if shift == 0:
                        kept[i, 0:BLOCK_ROWS] = block
                    else:
                        send[shift - 1, i, 0:BLOCK_ROWS] = block

        if shift == 0:
            kept[7, 0:1] = row
        else:
            send[shift - 1, 7, 0:1] = row


def inbox_kernel(ids, pull_group, owner, kept, from1, from2, from3, inbox, summed):
    group, slab = ids[0], ids[1]
    sources = (kept, from1, from2, from3)
    for slot in range(2):
        away = lax.rem(group - pull_group[group, 2 * slab + slot] + 4, 4)
        for shift in range(4):

            @pl.when(away == shift)
            def _():
                for i in range(7):
                    inbox[i, pl.ds(slot, BLOCK_ROWS, stride=2)] = sources[shift][i, 0:BLOCK_ROWS]

    row = jnp.zeros((1, LANES), F32)
    for shift in range(4):
        mine = owner[lax.rem(group - shift + 4, 4)] == group
        row = row + jnp.where(mine, sources[shift][7, 0:1], 0.0)
    summed[...] = row


def first_kernel(low, high, own, pull, e_own, p0, p1, p2, e, up, down, moments, d, stage):
    def gather(c):
        widen(low, (c,), p0, (c, 0))
        widen(low, (3 + c,), p0, (c, 1))
        widen(high, (3 + c,), p0, (c, 5))
        widen(high, (c,), p0, (c, 6))
        p0[c, 1] = p0[c, 1] + pull[c, 0]
        p0[c, 5] = p0[c, 5] - pull[c, 2]
        widen(low, (6 + c,), stage, (0,))
        widen(high, (6 + c,), stage, (1,))
        p0[c, 2] = own[c, 0] - stage[0]
        p0[c, 3] = own[c, 1]
        p0[c, 4] = own[c, 2] + stage[1]

    on_plane_loop(3, gather)
    widen(low, (9,), e, (0,))
    widen(low, (10,), e, (1,))
    widen(high, (10,), e, (5,))
    widen(high, (9,), e, (6,))
    for z in range(3):
        e[2 + z] = e_own[z]

    def step1(j):
        ee = three(e, j + 1)
        diag = diagonal(ee)
        d[j] = diag

        def each(c):
            p1[c, j] = operator(three(p0, c, j + 1), ee, diag)

        for c in range(3):
            each(c)

    on_plane_loop(5, step1)

    def step2(t, carry):
        c, z = t // 3, t % 3
        new = operator(three(p1, c, z + 1), three(e, z + 2), d[z + 1])
        p2[c, z] = new
        r0, r1 = p0[c, z + 2], p1[c, z + 1]
        terms = (r0 * r0, r0 * r1, r1 * r1, r1 * new, new * new)
        put(narrow(p2, (c, z)), (up, (3 * c + z,)), (down, (3 * c + z,)))
        return tuple(a + fold(v) for a, v in zip(carry, terms))

    zero = jnp.zeros((8, LANES), F32)
    sums = lax.fori_loop(0, 9, step2, (zero,) * 5)
    lane = lane_of(1)
    keep = lane_of(8) < NVX
    row = jnp.zeros((1, LANES), F32)
    for k in range(5):
        row = jnp.where(lane == k, total(jnp.where(keep, sums[k], 0.0)), row)
    moments[...] = jnp.broadcast_to(row, (32, LANES))

    def ship(c):
        put(narrow(p1, (c, 1)), (up, (9 + 2 * c,)))
        put(narrow(p1, (c, 2)), (up, (10 + 2 * c,)), (down, (10 + 2 * c,)))
        put(narrow(p1, (c, 3)), (down, (9 + 2 * c,)))
        put(narrow(p0, (c, 2)), (up, (15 + c,)))
        put(narrow(p0, (c, 4)), (down, (15 + c,)))

    on_plane_loop(3, ship)
    put(narrow(e, (2,)), (up, (18,)))
    put(narrow(e, (4,)), (down, (18,)))


def lanczos(table):
    row = jnp.sum(table, axis=0, keepdims=True)
    lane = lane_of(1)
    m0, m1, m2, m3, _ = [pick(row, lane, k) for k in range(5)]
    a0 = m1 / m0
    left = jnp.maximum(m2 - a0 * m1, 1e-7 * m2)
    a1 = jnp.clip((m3 - 2.0 * a0 * m2 + a0 * a0 * m1) / left, 0.0, 2.1)
    b1 = jnp.clip(left / m0, 0.0, 1.2)
    return a0, a1, b1


def second_kernel(moments, summed, low, high, p0, p1, p2, e_in, basis, gram, v2, v3, v4, e, d, v1, flat):
    a0, a1, b1 = lanczos(moments[...])
    c1, c0 = -(a0 + a1), a0 * a1 - b1

    widen(low, (18,), e, (0,))
    widen(high, (18,), e, (8,))
    for j in range(7):
        e[1 + j] = e_in[j]

    def gather(c):
        for side, ref, far, step in ((0, low, 0, 1), (1, high, 8, -1)):
            edge = 0 if side == 0 else 2
            inner = 1
            near = 2 if side == 0 else 0
            flat[0] = ref[3 * c + edge] + c1 * ref[(9 + 2 * c)] + c0 * ref[15 + c]
            flat[1] = ref[3 * c + inner] + c1 * ref[(10 + 2 * c)]
            widen(flat, (0,), v2, (c, far))
            widen(flat, (1,), v2, (c, far + step))
            widen(ref, (3 * c + near,), v2, (c, far + 2 * step))
            widen(ref, (10 + 2 * c,), v1, (c, 0 if side == 0 else 6))
        for j in range(1, 8):
            r0 = p0[c, j - 1]
            if j in (1, 7):
                v2[c, j] = v2[c, j] + c0 * r0
                v1[c, j - 1] = v1[c, j - 1] - a0 * r0
            else:
                r1 = p1[c, j - 2]
                base = v2[c, j] if j in (2, 6) else p2[c, j - 3]
                v2[c, j] = base + c1 * r1 + c0 * r0
                v1[c, j - 1] = r1 - a0 * r0

    on_plane_loop(3, gather)

    def step3(j):
        ee = three(e, j + 1)
        diag = diagonal(ee)
        d[j] = diag
        for c in range(3):
            u = three(v2, c, j + 1)
            v3[c, j] = operator(u, ee, diag) - a1 * u[1] - b1 * v1[c, j]

    on_plane_loop(7, step3)

    def step4(j):
        ee = three(e, j + 2)
        diag = d[j + 1]
        for c in range(3):
            u = three(v3, c, j + 1)
            v4[c, j] = operator(u, ee, diag) - a1 * u[1] - b1 * v2[c, j + 2]

    on_plane_loop(5, step4)

    def step5(t, carry):
        c, z = t // 3, t % 3
        u = three(v4, c, z + 1)
        new = operator(u, three(e, z + 3), d[z + 2])
        vectors = [p0[c, z + 2], v1[c, z + 2], v2[c, z + 3], v3[c, z + 2], u[1], new]
        for k in range(5):
            basis[k, c, z] = vectors[k]
        return tuple(a + fold(vectors[i] * vectors[j]) for a, (i, j) in zip(carry, PAIRS))

    zero = jnp.zeros((8, LANES), F32)
    sums = lax.fori_loop(0, 9, step5, (zero,) * len(PAIRS))
    lane = lane_of(1)
    keep = lane_of(8) < NVX
    row = pltpu.roll(jnp.broadcast_to(summed[...], (8, LANES)), SUM_BASE, 1)[0:1]
    for k in range(len(PAIRS)):
        row = jnp.where(lane == k, total(jnp.where(keep, sums[k], 0.0)), row)
    gram[...] = jnp.broadcast_to(row, (32, LANES))


def plus(x, y):
    return y if x is None else x if y is None else x + y


def times(x, y):
    return None if x is None or y is None else x * y


def inner(g, x, y):
    out = None
    for i in range(6):
        part = None
        for j in range(6):
            part = plus(part, times(g.get((min(i, j), max(i, j))), y[j]))
        out = plus(out, times(x[i], part))
    return out


def last_kernel(moments, gram, basis, correction, sums, wide):
    a0, a1, b1 = lanczos(moments[...])
    row = jnp.sum(gram[...], axis=0, keepdims=True)
    lane = lane_of(1)
    g = {pair: pick(row, lane, k) for k, pair in enumerate(PAIRS)}
    one = jnp.ones((1, 1), F32)

    def act(v):
        out = [None] * 6
        diag = (a0, a1, a1, a1, None)
        for i in range(5):
            out[i + 1] = plus(out[i + 1], v[i])
            out[i] = plus(out[i], times(diag[i], v[i]))
            if 1 <= i <= 3:
                out[i - 1] = plus(out[i - 1], times(b1, v[i]))
        return out

    found = [None] * 6
    residual = [one] + [None] * 5
    direction = [one] + [None] * 5
    norm = g[0, 0]
    for turn in range(5):
        image = act(direction)
        alpha = norm / inner(g, direction, image)
        found = [plus(x, times(alpha, v)) for x, v in zip(found, direction)]
        if turn < 4:
            residual = [plus(x, times(-alpha, v)) for x, v in zip(residual, image)]
            new = inner(g, residual, residual)
            beta = new / norm
            direction = [plus(x, times(beta, v)) for x, v in zip(residual, direction)]
            norm = new
    weights = [x * (1.0 / 16.0) for x in found[:5]]

    def plane(t):
        c, z = t // 3, t % 3
        out = weights[0] * basis[0, c, z]
        for k in range(1, 5):
            out = out + weights[k] * basis[k, c, z]
        wide[z] = out
        put(narrow(wide, (z,)), (correction, (c, z)))

    on_plane_loop(9, plane)

    bulk = pick(row, lane, SUM_BASE + BULK_LANE)
    coef = pick(row, lane, SUM_BASE + COEF_LANE)
    shifted = pltpu.roll(jnp.broadcast_to(row, (8, LANES)), LANES - SUM_BASE, 1)[0:1]
    entry = lane - 6
    i, j = entry // 6, entry % 6
    tangent = (lane >= 6) & (lane < 42)
    normal = tangent & (i < 3) & (j < 3)
    out = jnp.where(tangent, 2.0 * shifted, shifted)
    out = out + jnp.where(tangent & (i == j), 2.0 * coef, 0.0)
    out = out + jnp.where(normal, bulk - (2.0 / 3.0) * coef, 0.0)
    sums[...] = out


def shape(*dims):
    return jax.ShapeDtypeStruct(dims, F32)


VM = pl.BlockSpec(memory_space=pltpu.VMEM)
SM = pl.BlockSpec(memory_space=pltpu.SMEM)


def call(kernel, in_specs, outs, scratch, args, flops, name):
    size = sum(4 * math.prod(a.shape) for a in (*args, *outs))
    return pl.pallas_call(
        kernel,
        out_shape=tuple(outs),
        in_specs=in_specs,
        out_specs=(VM,) * len(outs),
        scratch_shapes=[pltpu.VMEM(s, F32) for s in scratch],
        compiler_params=pltpu.CompilerParams(vmem_limit_bytes=48 * 2**20),
        cost_estimate=pl.CostEstimate(flops=flops, bytes_accessed=size, transcendentals=0),
        name=name,
    )(*args)


def on_device(
    plastic_strain,
    hardening_var,
    strain_start,
    strain_step,
    shear_mod,
    bulk_mod,
    yield_stress,
    substeps,
    pull_group,
    pull_block,
    owner,
):
    slabs = lax.axis_size("slab")
    ids = jnp.stack([lax.axis_index("rve"), lax.axis_index("slab")]).astype(jnp.int32)
    six = [a.reshape(6, DEPTH, FLAT, LANES) for a in (plastic_strain, strain_start, strain_step)]
    one = [a.reshape(DEPTH, FLAT, LANES) for a in (hardening_var, shear_mod, bulk_mod, yield_stress)]
    plane = (FLAT, LANES)
    wide = (NVX, LANES)

    up, down, own, pull, e_own, history, dev, extra = call(
        map_kernel,
        [SM, SM] + [VM] * 7,
        [
            shape(UP_A, *plane),
            shape(UP_A, *plane),
            shape(3, 3, *wide),
            shape(3, 3, *wide),
            shape(3, *wide),
            shape(7, 3, *plane),
            shape(6, 3, *plane),
            shape(3, 3, *plane),
        ],
        [(7, *plane), (7, *wide)],
        (ids, substeps, six[0], one[0], six[1], six[2], one[1], one[2], one[3]),
        5_000_000,
        "return_map",
    )
    forward = [(i, (i + 1) % slabs) for i in range(slabs)]
    backward = [((i + 1) % slabs, i) for i in range(slabs)]
    low = lax.ppermute(up, "slab", forward)
    high = lax.ppermute(down, "slab", backward)

    send, kept = call(
        sums_kernel,
        [SM, SM, SM] + [VM] * 4,
        [shape(3, 8, 24, LANES), shape(8, 24, LANES)],
        [],
        (ids, pull_group, pull_block, dev, extra, one[2], history),
        2_000_000,
        "element_partials",
    )
    came = [
        lax.ppermute(send[k - 1], "rve", [(i, (i + k) % 4) for i in range(4)]) for k in (1, 2, 3)
    ]

    p0, p1, p2, e, up2, down2, moments = call(
        first_kernel,
        [VM] * 5,
        [
            shape(3, 7, *wide),
            shape(3, 5, *wide),
            shape(3, 3, *wide),
            shape(7, *wide),
            shape(UP_B, *plane),
            shape(UP_B, *plane),
            shape(32, LANES),
        ],
        [(5, *wide), (2, *wide)],
        (low, high, own, pull, e_own),
        5_000_000,
        "basis_first",
    )
    low2 = lax.ppermute(up2, "slab", forward)
    high2 = lax.ppermute(down2, "slab", backward)
    inbox, summed = call(
        inbox_kernel,
        [SM, SM, SM] + [VM] * 4,
        [shape(7, 2 * BLOCK_ROWS, LANES), shape(1, LANES)],
        [],
        (ids, pull_group, owner, kept, *came),
        100_000,
        "inbox",
    )
    moments = lax.all_to_all(moments, "slab", split_axis=0, concat_axis=0, tiled=True)
    basis, gram = call(
        second_kernel,
        [VM] * 8,
        [shape(5, 3, 3, *wide), shape(32, LANES)],
        [
            (3, 9, *wide),
            (3, 7, *wide),
            (3, 5, *wide),
            (9, *wide),
            (7, *wide),
            (3, 7, *wide),
            (2, *plane),
        ],
        (moments, summed, low2, high2, p0, p1, p2, e),
        8_000_000,
        "basis_second",
    )
    gram = lax.all_to_all(gram, "slab", split_axis=0, concat_axis=0, tiled=True)
    correction, element = call(
        last_kernel,
        [VM] * 3,
        [shape(3, 3, *plane), shape(1, LANES)],
        [(3, *wide)],
        (moments, gram, basis),
        1_000_000,
        "combine",
    )
    inbox = inbox.reshape(7, BLOCK_ROWS, 2, LANES).transpose(0, 2, 1, 3)
    return (
        correction.reshape(3, 1, DEPTH, FLAT * LANES),
        inbox.reshape(7, 1, 2, BLOCK_ROWS * LANES),
        element[:, :42],
    )


def solution(mesh):
    return jax.shard_map(
        on_device,
        mesh=mesh,
        in_specs=(
            P(None, "rve", "slab", None),
            P("rve", "slab", None),
            P(None, "rve", "slab", None),
            P(None, "rve", "slab", None),
            P("rve", "slab", None),
            P("rve", "slab", None),
            P("rve", "slab", None),
            P(),
            P(),
            P(),
            P(),
        ),
        out_specs=(P(None, "rve", "slab", None), P(None, "rve", "slab", None), P("rve", None)),
        check_vma=False,
    )
```

```python
import math

import jax
import jax.numpy as jnp
from jax import lax
from jax.experimental import pallas as pl
from jax.experimental.pallas import tpu as pltpu
from jax.sharding import PartitionSpec as P

NVX = 96
LANES = 128
FLAT = 72
DEPTH = 3
BLOCK_ROWS = 18
BLOCKS = 12
VOXELS = 884736.0
F32 = jnp.float32

root_two_thirds = math.sqrt(2.0 / 3.0)
half_root = 1.0 / math.sqrt(2.0)
RETURN = 2.0 / 2.2
HARDEN = 0.2 / 2.2

BULK_LANE = 42
COEF_LANE = 43
SUM_BASE = 64
PAIRS = [(i, j) for i in range(6) for j in range(i, 6) if (i, j) != (5, 5)]

UP_A = 11
UP_B = 19


def roll(values, shift, axis):
    return pltpu.roll(values, shift % values.shape[axis], axis)


def lane_of(rows):
    return lax.broadcasted_iota(jnp.int32, (rows, LANES), 1)


def widen(flat_ref, at, wide_ref, to):
    lane = lane_of(24)
    x = jnp.where(lane < 96, lane, jnp.where(lane < 112, lane - 96, lane - 32))
    a = [flat_ref[(*at, pl.ds(i, 24, stride=3), slice(None))] for i in range(3)]

    def take(i, place):
        return jnp.take_along_axis(a[i], place & 127, axis=1, mode="promise_in_bounds")

    second, third, last = 96 + x, 192 + x, 288 + x
    rows = [
        take(0, x),
        jnp.where(second < 128, take(0, second), take(1, second)),
        jnp.where(third < 256, take(1, third), take(2, third)),
        take(2, last),
    ]
    for i, row in enumerate(rows):
        wide_ref[(*to, pl.ds(i, 24, stride=4), slice(None))] = row


def narrow(wide_ref, at):
    lane = lane_of(24)
    o0, o1, o2, o3 = [wide_ref[(*at, pl.ds(i, 24, stride=4), slice(None))] for i in range(4)]
    r1, r2, r3 = roll(o1, 96, 1), roll(o2, 64, 1), roll(o3, 32, 1)
    return (
        jnp.where(lane < 96, o0, r1),
        jnp.where(lane < 64, r1, r2),
        jnp.where(lane < 32, r2, r3),
    )


def put(rows, *targets):
    for ref, to in targets:
        for i in range(3):
            ref[(*to, pl.ds(i, 24, stride=3), slice(None))] = rows[i]


def along(values, axis):
    values = values + roll(values, 1, axis)
    return values + roll(values, -1, axis)


def operator(u, e, turned, d):
    mid = e[1] * u[1]
    once = along((u[0] + u[2]) + (u[1] + u[1]), 0)
    twice = along((e[0] * u[0] + e[2] * u[2]) + (mid + mid), 0)
    both = e[1] * once + twice
    sides = roll(turned[0] * once + twice, -1, 1) + roll(turned[1] * once + twice, 1, 1)
    return d * u[1] - (both + both) - sides


def diagonal(e):
    return 64.4 * e[1] + along(along((e[0] + e[2]) + (e[1] + e[1]), 0), 1)


def prepare(j, e, d, turned):
    d[j] = diagonal(e)
    turned[0, j] = roll(e[1], 1, 1)
    turned[1, j] = roll(e[1], -1, 1)


def three(ref, *at):
    *lead, mid = at
    return [ref[(*lead, mid + k)] for k in (-1, 0, 1)]


def total(values):
    return jnp.sum(jnp.sum(values, axis=0, keepdims=True), axis=1, keepdims=True)


def fold(values):
    out = values[0:8]
    for i in range(8, values.shape[0], 8):
        out = out + values[i : i + 8]
    return out


def pick(row, lane, k):
    return jnp.sum(jnp.where(lane == k, row, 0.0), axis=1, keepdims=True)


def on_plane_loop(count, body):
    lax.fori_loop(0, count, lambda i, c: (body(i), c)[1], 0)


def map_kernel(
    ids,
    counts_in,
    *refs,
):
    _map_kernel(ids, counts_in, refs[:7], *refs[7:])


def _map_kernel(
    ids,
    counts_in,
    sources,
    up,
    down,
    own,
    pull,
    e_wide,
    history,
    dev,
    extra,
    flat,
    wide,
    counts,
    plastic,
    hard,
    begin,
    delta,
    shear,
    bulk,
    yields,
    count_sem,
    sems,
):
    def copies(z):
        out = []
        for k, (source, target) in enumerate(zip(sources, targets)):
            at = (slice(None), z) if len(source.shape) == 4 else (z,)
            out.append(pltpu.make_async_copy(source.at[at], target.at[at], sems.at[z, k]))
        return out

    targets = (plastic, hard, begin, delta, shear, bulk, yields)
    get_counts = pltpu.make_async_copy(counts_in, counts, count_sem)
    get_counts.start()
    for z in range(DEPTH):
        for copy in copies(z):
            copy.start()
    get_counts.wait()
    group, first = ids[0], ids[1] * BLOCKS
    row = lax.broadcasted_iota(jnp.int32, (FLAT, LANES), 0)

    def plane(z):
        for copy in copies(z):
            copy.wait()
        block = [counts[group, first + 4 * z + b] for b in range(4)]
        turns = jnp.maximum(jnp.maximum(block[0], block[1]), jnp.maximum(block[2], block[3]))
        held = jnp.where(
            row < 2 * BLOCK_ROWS,
            jnp.where(row < BLOCK_ROWS, block[0], block[1]),
            jnp.where(row < 3 * BLOCK_ROWS, block[2], block[3]),
        )
        share = 1.0 / held.astype(F32)
        twice_mu = 2.0 * shear[z]
        elastic = [begin[i, z] - plastic[i, z] for i in range(6)]
        step = [delta[i, z] for i in range(6)]
        third0 = (elastic[0] + elastic[1] + elastic[2]) * (1.0 / 3.0)
        third1 = (step[0] + step[1] + step[2]) * (1.0 / 3.0)
        stress = [twice_mu * (elastic[i] - third0 if i < 3 else elastic[i]) for i in range(6)]
        rate = twice_mu * share
        for i in range(6):
            flat[i] = rate * (step[i] - third1 if i < 3 else step[i])
        floor = root_two_thirds * yields[z]
        limit0 = floor + (root_two_thirds * 0.15) * twice_mu * hard[z]
        most = 1.0 / floor

        def substep(t, carry):
            *s, gone, _, _ = carry
            act = jnp.where(held >= turns - t, 1.0, 0.0)
            s = [s[i] + act * flat[i] for i in range(6)]
            square = s[0] * s[0]
            for i in range(1, 6):
                square = square + s[i] * s[i]
            square = jnp.maximum(square, 1e-30)
            inverse = lax.rsqrt(square)
            over = jnp.maximum(square * inverse - (limit0 + HARDEN * gone), 0.0) * act
            inverse = jnp.minimum(inverse, most)
            theta = 1.0 - (RETURN * over) * inverse
            return (*[theta * s[i] for i in range(6)], gone + over, theta, inverse)

        zero = jnp.zeros((FLAT, LANES), F32)
        *s, gone, theta, inverse = lax.fori_loop(0, turns, substep, (*stress, zero, zero, zero))
        mu = 0.5 * twice_mu
        per = 1.0 / twice_mu
        elastic = [begin[i, z] - plastic[i, z] + delta[i, z] for i in range(6)]
        trace = elastic[0] + elastic[1] + elastic[2]
        third = trace * (1.0 / 3.0)
        for i in range(6):
            whole = elastic[i] - third if i < 3 else elastic[i]
            history[i, z] = plastic[i, z] + (whole - per * s[i])
            dev[i, z] = s[i]
        history[6, z] = hard[z] + (root_two_thirds / 1.1) * per * gone
        pressure = bulk[z] * trace
        ratio = inverse / theta
        coef = mu * theta
        extra[0, z] = pressure
        extra[1, z] = mu * (theta - 1.0) * (ratio * ratio)
        extra[2, z] = coef
        for i in range(6):
            flat[i] = pressure + s[i] if i < 3 else s[i]
        flat[6] = coef * (1.0 / 128.0)
        for i in range(7):
            widen(flat, (i,), wide, (i,))
        e_wide[z] = wide[6]

        def along_x(u):
            return roll(u, -1, 1) - roll(u, 1, 1)

        def along_y(u):
            return roll(u, -1, 0) - roll(u, 1, 0)

        half = 0.5 * half_root
        own[0, z] = 0.5 * along_x(wide[0]) + half * along_y(wide[5])
        own[1, z] = half * along_x(wide[5]) + 0.5 * along_y(wide[1])
        own[2, z] = half * (along_x(wide[4]) + along_y(wide[3]))
        pull[0, z] = half * wide[4]
        pull[1, z] = half * wide[3]
        pull[2, z] = 0.5 * wide[2]

    on_plane_loop(DEPTH, plane)

    for c in range(3):
        own[c, 0] = own[c, 0] + pull[c, 1]
        own[c, 1] = own[c, 1] + pull[c, 2] - pull[c, 0]
        own[c, 2] = own[c, 2] - pull[c, 1]
        for ref, z in ((up, 2), (down, 0)):
            ref[c] = own[c, 1]
            ref[3 + c] = own[c, z]
            ref[6 + c] = pull[c, z]
    for ref, z in ((up, 2), (down, 0)):
        ref[9] = e_wide[1]
        ref[10] = e_wide[z]


def sums_kernel(ids, pull_group, pull_block, dev, extra, bulk, history, *sends):
    group, slab = ids[0], ids[1]
    lane = lane_of(1)
    pairs = [(i, j) for i in range(6) for j in range(i, 6)]

    def chunk(t, carry):
        z, at = t // 3, pl.multiple_of((t % 3) * 24, 8)
        rows = pl.ds(at, 24)
        s = [dev[i, z, rows] for i in range(6)]
        pressure = extra[0, z, rows]
        weighted = extra[1, z, rows]
        terms = [pressure + s[i] if i < 3 else s[i] for i in range(6)]
        terms += [bulk[z, rows], extra[2, z, rows]]
        ws = [weighted * v for v in s]
        terms += [ws[i] * s[j] for i, j in pairs]
        return tuple(c + fold(v) for c, v in zip(carry, terms))

    zero = jnp.zeros((8, LANES), F32)
    sums = lax.fori_loop(0, 9, chunk, (zero,) * (8 + len(pairs)))
    sums = [total(v) * (1.0 / VOXELS) for v in sums]
    row = jnp.zeros((1, LANES), F32)
    for i in range(6):
        row = jnp.where(lane == i, sums[i], row)
    row = jnp.where(lane == BULK_LANE, sums[6], row)
    row = jnp.where(lane == COEF_LANE, sums[7], row)
    for k, (i, j) in enumerate(pairs):
        hit = (lane == 6 + 6 * i + j) | (lane == 6 + 6 * j + i)
        row = jnp.where(hit, sums[8 + k], row)

    for shift in range(4):
        to = lax.rem(group + shift, 4)
        first = pull_group[to, 2 * slab] == group
        at = jnp.where(first, pull_block[to, 2 * slab], pull_block[to, 2 * slab + 1])
        at = jnp.clip(at - slab * BLOCKS, 0, BLOCKS - 1)
        z, part = at // 4, at % 4
        for b in range(4):

            @pl.when(part == b)
            def _():
                for i in range(7):
                    block = history[i, z, pl.ds(BLOCK_ROWS * b, BLOCK_ROWS)]
                    sends[shift][i, 0:BLOCK_ROWS] = block

        sends[shift][7, 0:1] = row


def inbox_kernel(ids, pull_group, owner, kept, from1, from2, from3, inbox, summed):
    group, slab = ids[0], ids[1]
    sources = (kept, from1, from2, from3)
    for slot in range(2):
        away = lax.rem(group - pull_group[group, 2 * slab + slot] + 4, 4)
        for shift in range(4):

            @pl.when(away == shift)
            def _():
                for i in range(7):
                    inbox[i, pl.ds(slot, BLOCK_ROWS, stride=2)] = sources[shift][i, 0:BLOCK_ROWS]

    row = jnp.zeros((1, LANES), F32)
    for shift in range(4):
        mine = owner[lax.rem(group - shift + 4, 4)] == group
        row = row + jnp.where(mine, sources[shift][7, 0:1], 0.0)
    summed[...] = row


def first_kernel(low, high, own, pull, e_own, *refs):
    basis_first(low, high, own, pull, e_own, *refs[3:])


def basis_first(low, high, own, pull, e_own, p0, p1, p2, e, up, down, moments, d, turned, sems):
    used = [0]

    def ship(source, *targets):
        out = []
        for target in targets:
            out.append(pltpu.make_async_copy(source, target, sems.at[used[0]]))
            used[0] += 1
            out[-1].start()
        return out

    for c in range(3):
        p0[c, 0] = low[c]
        p0[c, 1] = low[3 + c] + pull[c, 0]
        p0[c, 2] = own[c, 0] - low[6 + c]
        p0[c, 3] = own[c, 1]
        p0[c, 4] = own[c, 2] + high[6 + c]
        p0[c, 5] = high[3 + c] - pull[c, 2]
        p0[c, 6] = high[c]
    for j, plane in enumerate((low[9], low[10], e_own[0], e_own[1], e_own[2], high[10], high[9])):
        e[j] = plane
    copies = ship(p0.at[:, 2], up.at[pl.ds(15, 3)]) + ship(p0.at[:, 4], down.at[pl.ds(15, 3)])
    copies += ship(e.at[2], up.at[18]) + ship(e.at[4], down.at[18])

    def step1(j):
        ee = three(e, j + 1)
        prepare(j, ee, d, turned)
        sides = (turned[0, j], turned[1, j])
        for c in range(3):
            p1[c, j] = operator(three(p0, c, j + 1), ee, sides, d[j])

    on_plane_loop(5, step1)
    copies += ship(p1.at[:, 1], up.at[pl.ds(9, 3)]) + ship(p1.at[:, 3], down.at[pl.ds(9, 3)])
    copies += ship(p1.at[:, 2], up.at[pl.ds(12, 3)], down.at[pl.ds(12, 3)])

    def step2(z, carry):
        ee = three(e, z + 2)
        sides = (turned[0, z + 1], turned[1, z + 1])
        for c in range(3):
            new = operator(three(p1, c, z + 1), ee, sides, d[z + 1])
            p2[z, c] = new
            r0, r1 = p0[c, z + 2], p1[c, z + 1]
            terms = (r0 * r0, r0 * r1, r1 * r1, r1 * new)
            carry = tuple(a + fold(v) for a, v in zip(carry, terms))
        return carry

    zero = jnp.zeros((8, LANES), F32)
    sums = lax.fori_loop(0, 3, step2, (zero,) * 4)
    for z in range(3):
        rows = pl.ds(3 * z, 3)
        copies += ship(p2.at[z], up.at[rows], down.at[rows])
    lane = lane_of(1)
    keep = lane_of(8) < NVX
    row = jnp.zeros((1, LANES), F32)
    for k in range(4):
        row = jnp.where(lane == k, total(jnp.where(keep, sums[k], 0.0)), row)
    moments[...] = row
    for copy in copies:
        copy.wait()


def lanczos(m0, m1, m2, m3):
    over = jnp.where(m0 > 0.0, m0, 1.0)
    a0 = jnp.clip(m1 / over, 0.0, 2.1)
    left = jnp.maximum(m2 - 2.0 * a0 * m1 + a0 * a0 * m0, 1e-7 * m2)
    b1 = jnp.clip(left / over, 0.0, 1.2)
    left = jnp.where(left > 0.0, left, 1.0)
    a1 = jnp.clip((m3 - 2.0 * a0 * m2 + a0 * a0 * m1) / left, 0.0, 2.1)
    return a0, a1, b1


def second_kernel(moments, summed, low, high, p0, p1, p2, e_in, basis, gram, v2, v3, v4, e, d, v1, turned):
    lane = lane_of(1)
    found = [pick(moments[...], lane, k) for k in range(4)]
    a0, a1, b1 = lanczos(*found)
    c1, c0 = -(a0 + a1), a0 * a1 - b1
    for j in range(7):
        e[1 + j] = e_in[j]
    e[0] = low[18]
    e[8] = high[18]
    for c in range(3):
        for ref, edge, inward in ((low, 0, 1), (high, 8, -1)):
            order = (0, 3, 6)[::inward]
            second, third = edge + inward, edge + 2 * inward
            r0 = p0[c, second - 1]
            v2[c, edge] = ref[order[0] + c] + c1 * ref[9 + c] + c0 * ref[15 + c]
            v2[c, second] = ref[order[1] + c] + c1 * ref[12 + c] + c0 * r0
            v1[c, second - 1] = ref[12 + c] - a0 * r0
            r0, r1 = p0[c, third - 1], p1[c, third - 2]
            v2[c, third] = ref[order[2] + c] + c1 * r1 + c0 * r0
            v1[c, third - 1] = r1 - a0 * r0
        for z in range(3):
            r0, r1 = p0[c, z + 2], p1[c, z + 1]
            v2[c, z + 3] = p2[z, c] + c1 * r1 + c0 * r0
            v1[c, z + 2] = r1 - a0 * r0

    def step3(j):
        ee = three(e, j + 1)
        prepare(j, ee, d, turned)
        sides = (turned[0, j], turned[1, j])
        for c in range(3):
            u = three(v2, c, j + 1)
            v3[c, j] = operator(u, ee, sides, d[j]) - a1 * u[1] - b1 * v1[c, j]

    on_plane_loop(7, step3)

    def step4(j):
        ee = three(e, j + 2)
        sides = (turned[0, j + 1], turned[1, j + 1])
        for c in range(3):
            u = three(v3, c, j + 1)
            v4[c, j] = operator(u, ee, sides, d[j + 1]) - a1 * u[1] - b1 * v2[c, j + 2]

    on_plane_loop(5, step4)

    def step5(z, carry):
        ee = three(e, z + 3)
        sides = (turned[0, z + 2], turned[1, z + 2])
        for c in range(3):
            u = three(v4, c, z + 1)
            new = operator(u, ee, sides, d[z + 2])
            vectors = [p0[c, z + 2], v1[c, z + 2], v2[c, z + 3], v3[c, z + 2], u[1], new]
            for k in range(5):
                basis[k, c, z] = vectors[k]
            carry = tuple(a + fold(vectors[i] * vectors[j]) for a, (i, j) in zip(carry, PAIRS))
        return carry

    zero = jnp.zeros((8, LANES), F32)
    sums = lax.fori_loop(0, 3, step5, (zero,) * len(PAIRS))
    keep = lane_of(8) < NVX
    row = pltpu.roll(jnp.broadcast_to(summed[...], (8, LANES)), SUM_BASE, 1)[0:1]
    sent = [total(jnp.where(keep, v, 0.0)) for v in sums] + [a0, a1, b1] + found
    for k, value in enumerate(sent):
        row = jnp.where(lane == k, value, row)
    gram[...] = jnp.broadcast_to(row, (32, LANES))


def plus(x, y):
    return y if x is None else x if y is None else x + y


def times(x, y):
    if x is None or y is None:
        return None
    return y if isinstance(x, float) else x if isinstance(y, float) else x * y


def inner(g, x, y):
    out = None
    for i in range(6):
        part = None
        for j in range(6):
            part = plus(part, times(g.get((min(i, j), max(i, j))), y[j]))
        out = plus(out, times(x[i], part))
    return out


def minus(x, y):
    return x if y is None else -y if x is None else x - y


def basis_change(own, common):
    a0, a1, b1 = own
    c0, c1, d1 = common
    diag = (a0, a1, a1, a1)
    rows = [[1.0] + [None] * 5, [a0 - c0, 1.0] + [None] * 4]
    for k in range(1, 4):
        last, before, row = rows[k], rows[k - 1], [None] * 6
        for j in range(k + 2):
            value = last[j - 1] if j >= 1 else None
            if j <= 3 and last[j] is not None:
                value = plus(value, times(diag[j] - c1, last[j]))
            if j <= 2:
                value = plus(value, times(b1, last[j + 1]))
            row[j] = minus(value, times(d1, before[j]))
        rows.append(row)
    last, row = rows[4], [None] * 6
    for j in range(5):
        row[j + 1] = plus(row[j + 1], last[j])
        if j <= 3:
            row[j] = plus(row[j], times(diag[j], last[j]))
        if 1 <= j <= 3:
            row[j - 1] = plus(row[j - 1], times(b1, last[j]))
    return rows + [row]


def last_kernel(ids, gram, basis, correction, sums, wide):
    table = gram[...]
    row = jnp.sum(table, axis=0, keepdims=True)
    lane = lane_of(1)
    sides = jnp.concatenate([table, jnp.zeros((LANES - 32, LANES), F32)], axis=0).T
    entry = [sides[k : k + 1] for k in range(len(PAIRS) + 7)]
    own = entry[len(PAIRS) : len(PAIRS) + 3]
    a0, a1, b1 = lanczos(*[jnp.sum(v, axis=1, keepdims=True) for v in entry[len(PAIRS) + 3 :]])
    change = basis_change(own, (a0, a1, b1))
    local = {pair: entry[k] for k, pair in enumerate(PAIRS)}

    def dot(x, y):
        out = None
        for u, v in zip(x, y):
            out = plus(out, times(u, v))
        return out

    half = [[dot(change[k], [local.get((min(j, m), max(j, m))) for j in range(6)]) for m in range(6)] for k in range(5)]
    g = {(k, m): jnp.sum(dot(half[k], change[m]), axis=1, keepdims=True) for k, m in PAIRS}
    one = jnp.ones((1, 1), F32)

    def act(v):
        out = [None] * 6
        diag = (a0, a1, a1, a1, None)
        for i in range(5):
            out[i + 1] = plus(out[i + 1], v[i])
            out[i] = plus(out[i], times(diag[i], v[i]))
            if 1 <= i <= 3:
                out[i - 1] = plus(out[i - 1], times(b1, v[i]))
        return out

    found = [None] * 6
    residual = [one] + [None] * 5
    direction = [one] + [None] * 5
    norm = g[0, 0]
    for turn in range(5):
        image = act(direction)
        alpha = norm / inner(g, direction, image)
        found = [plus(x, times(alpha, v)) for x, v in zip(found, direction)]
        if turn < 4:
            residual = [plus(x, times(-alpha, v)) for x, v in zip(residual, image)]
            new = inner(g, residual, residual)
            beta = new / norm
            direction = [plus(x, times(beta, v)) for x, v in zip(residual, direction)]
            norm = new
    weights = []
    for j in range(5):
        value = jnp.broadcast_to(dot(found[:5], [change[k][j] for k in range(5)]), (1, LANES))
        weights.append(pick(value, lane, ids[1]) * (1.0 / 16.0))

    def plane(z):
        for c in range(3):
            out = weights[0] * basis[0, c, z]
            for k in range(1, 5):
                out = out + weights[k] * basis[k, c, z]
            wide[c] = out
            put(narrow(wide, (c,)), (correction, (c, z)))

    on_plane_loop(DEPTH, plane)

    bulk = pick(row, lane, SUM_BASE + BULK_LANE)
    coef = pick(row, lane, SUM_BASE + COEF_LANE)
    shifted = pltpu.roll(jnp.broadcast_to(row, (8, LANES)), LANES - SUM_BASE, 1)[0:1]
    entry = lane - 6
    i, j = entry // 6, entry % 6
    tangent = (lane >= 6) & (lane < 42)
    normal = tangent & (i < 3) & (j < 3)
    out = jnp.where(tangent, 2.0 * shifted, shifted)
    out = out + jnp.where(tangent & (i == j), 2.0 * coef, 0.0)
    out = out + jnp.where(normal, bulk - (2.0 / 3.0) * coef, 0.0)
    sums[...] = out


def shape(*dims):
    return jax.ShapeDtypeStruct(dims, F32)


def near(*dims):
    return pltpu.VMEM(dims, F32)


def far(*dims):
    return pltpu.HBM(dims, F32)


def in_hbm(array):
    return pltpu.with_memory_space_constraint(array, pltpu.HBM)


VM = pl.BlockSpec(memory_space=pltpu.VMEM)
SM = pl.BlockSpec(memory_space=pltpu.SMEM)
HB = pl.BlockSpec(memory_space=pltpu.HBM)
ANY = pl.BlockSpec(memory_space=pl.ANY)


def call(kernel, in_specs, outs, scratch, args, flops, name, limit=12, out_specs=None):
    size = sum(4 * math.prod(a.shape) for a in (*args, *outs))
    return pl.pallas_call(
        kernel,
        out_shape=tuple(outs),
        in_specs=in_specs,
        out_specs=tuple(out_specs or (VM,) * len(outs)),
        scratch_shapes=[pltpu.VMEM(s, F32) if isinstance(s, tuple) else s for s in scratch],
        compiler_params=pltpu.CompilerParams(vmem_limit_bytes=limit * 2**20),
        cost_estimate=pl.CostEstimate(flops=flops, bytes_accessed=size, transcendentals=0),
        name=name,
    )(*args)


def on_device(
    plastic_strain,
    hardening_var,
    strain_start,
    strain_step,
    shear_mod,
    bulk_mod,
    yield_stress,
    substeps,
    pull_group,
    pull_block,
    owner,
):
    slabs = lax.axis_size("slab")
    ids = jnp.stack([lax.axis_index("rve"), lax.axis_index("slab")]).astype(jnp.int32)
    six = [a.reshape(6, DEPTH, FLAT, LANES) for a in (plastic_strain, strain_start, strain_step)]
    one = [a.reshape(DEPTH, FLAT, LANES) for a in (hardening_var, shear_mod, bulk_mod, yield_stress)]
    plane = (FLAT, LANES)
    wide = (NVX, LANES)

    up, down, own, pull, e_own, history, dev, extra = call(
        map_kernel,
        [SM] + [HB] * 8,
        [
            shape(UP_A, *wide),
            shape(UP_A, *wide),
            shape(3, 3, *wide),
            shape(3, 3, *wide),
            shape(3, *wide),
            shape(7, 3, *plane),
            shape(6, 3, *plane),
            shape(3, 3, *plane),
        ],
        [
            pltpu.VMEM((7, *plane), F32),
            pltpu.VMEM((7, *wide), F32),
            pltpu.SMEM((4, 384), jnp.int32),
            pltpu.VMEM((6, DEPTH, *plane), F32),
            pltpu.VMEM((DEPTH, *plane), F32),
            pltpu.VMEM((6, DEPTH, *plane), F32),
            pltpu.VMEM((6, DEPTH, *plane), F32),
            pltpu.VMEM((DEPTH, *plane), F32),
            pltpu.VMEM((DEPTH, *plane), F32),
            pltpu.VMEM((DEPTH, *plane), F32),
            pltpu.SemaphoreType.DMA,
            pltpu.SemaphoreType.DMA((DEPTH, 7)),
        ],
        (ids, *map(in_hbm, (substeps, six[0], one[0], six[1], six[2], one[1], one[2], one[3]))),
        5_000_000,
        "return_map",
    )
    forward = [(i, (i + 1) % slabs) for i in range(slabs)]
    backward = [((i + 1) % slabs, i) for i in range(slabs)]
    low = lax.ppermute(up, "slab", forward)
    high = lax.ppermute(down, "slab", backward)

    kept, *sends = call(
        sums_kernel,
        [SM, SM, SM] + [VM] * 4,
        [shape(8, 24, LANES)] * 4,
        [],
        (ids, pull_group, pull_block, dev, extra, one[2], history),
        2_000_000,
        "element_partials",
    )
    came = [
        lax.ppermute(sends[k - 1], "rve", [(i, (i + k) % 4) for i in range(4)]) for k in (1, 2, 3)
    ]

    p0, p1, p2, e, up2, down2, moments = call(
        first_kernel,
        [VM] * 5 + [ANY] * 3,
        [
            shape(3, 7, *wide),
            shape(3, 5, *wide),
            shape(3, 3, *wide),
            shape(7, *wide),
            shape(UP_B, *wide),
            shape(UP_B, *wide),
            shape(1, LANES),
        ],
        [(5, *wide), (2, 5, *wide), pltpu.SemaphoreType.DMA((14,))],
        (low, high, own, pull, e_own, *came),
        5_000_000,
        "basis_first",
    )
    low2 = lax.ppermute(up2, "slab", forward)
    high2 = lax.ppermute(down2, "slab", backward)
    inbox, summed = call(
        inbox_kernel,
        [SM, SM, SM] + [VM] * 4,
        [shape(7, 2 * BLOCK_ROWS, LANES), shape(1, LANES)],
        [],
        (ids, pull_group, owner, kept, *came),
        100_000,
        "inbox",
    )
    basis, gram = call(
        second_kernel,
        [VM] * 8,
        [shape(5, 3, 3, *wide), shape(32, LANES)],
        [
            (3, 9, *wide),
            (3, 7, *wide),
            (3, 5, *wide),
            (9, *wide),
            (7, *wide),
            (3, 7, *wide),
            (2, 7, *wide),
        ],
        (moments, summed, low2, high2, p0, p1, p2, e),
        8_000_000,
        "basis_second",
    )
    gram = lax.all_to_all(gram, "slab", split_axis=0, concat_axis=0, tiled=True)
    correction, element = call(
        last_kernel,
        [SM, VM, VM],
        [shape(3, 3, *plane), shape(1, LANES)],
        [(3, *wide)],
        (ids, gram, basis),
        1_000_000,
        "combine",
    )
    inbox = inbox.reshape(7, BLOCK_ROWS, 2, LANES).transpose(0, 2, 1, 3)
    return (
        correction.reshape(3, 1, DEPTH, FLAT * LANES),
        inbox.reshape(7, 1, 2, BLOCK_ROWS * LANES),
        element[:, :42],
    )


def solution(mesh):
    return jax.shard_map(
        on_device,
        mesh=mesh,
        in_specs=(
            P(None, "rve", "slab", None),
            P("rve", "slab", None),
            P(None, "rve", "slab", None),
            P(None, "rve", "slab", None),
            P("rve", "slab", None),
            P("rve", "slab", None),
            P("rve", "slab", None),
            P(),
            P(),
            P(),
            P(),
        ),
        out_specs=(P(None, "rve", "slab", None), P(None, "rve", "slab", None), P("rve", None)),
        check_vma=False,
    )
```

```python
import math

import jax
import jax.numpy as jnp
from jax import lax
from jax.experimental import pallas as pl
from jax.experimental.pallas import tpu as pltpu
from jax.sharding import PartitionSpec as P

NVX = 96
LANES = 128
FLAT = 72
DEPTH = 3
BLOCK_ROWS = 18
BLOCKS = 12
VOXELS = 884736.0
F32 = jnp.float32

root_two_thirds = math.sqrt(2.0 / 3.0)
half_root = 1.0 / math.sqrt(2.0)
RETURN = 2.0 / 2.2
HARDEN = 0.2 / 2.2

BULK_LANE = 42
COEF_LANE = 43
SUM_BASE = 64
PAIRS = [(i, j) for i in range(6) for j in range(i, 6) if (i, j) != (5, 5)]

FIRST = 12
SECOND = 11


def roll(values, shift, axis):
    return pltpu.roll(values, shift % values.shape[axis], axis)


def lane_of(rows):
    return lax.broadcasted_iota(jnp.int32, (rows, LANES), 1)


def widen(flat_ref, at, wide_ref, to):
    lane = lane_of(24)
    x = jnp.where(lane < 96, lane, jnp.where(lane < 112, lane - 96, lane - 32))
    a = [flat_ref[(*at, pl.ds(i, 24, stride=3), slice(None))] for i in range(3)]

    def take(i, place):
        return jnp.take_along_axis(a[i], place & 127, axis=1, mode="promise_in_bounds")

    second, third, last = 96 + x, 192 + x, 288 + x
    rows = [
        take(0, x),
        jnp.where(second < 128, take(0, second), take(1, second)),
        jnp.where(third < 256, take(1, third), take(2, third)),
        take(2, last),
    ]
    for i, row in enumerate(rows):
        wide_ref[(*to, pl.ds(i, 24, stride=4), slice(None))] = row


def narrow(wide_ref, at):
    lane = lane_of(24)
    o0, o1, o2, o3 = [wide_ref[(*at, pl.ds(i, 24, stride=4), slice(None))] for i in range(4)]
    r1, r2, r3 = roll(o1, 96, 1), roll(o2, 64, 1), roll(o3, 32, 1)
    return (
        jnp.where(lane < 96, o0, r1),
        jnp.where(lane < 64, r1, r2),
        jnp.where(lane < 32, r2, r3),
    )


def put(rows, *targets):
    for ref, to in targets:
        for i in range(3):
            ref[(*to, pl.ds(i, 24, stride=3), slice(None))] = rows[i]


def along(values, axis):
    values = values + roll(values, 1, axis)
    return values + roll(values, -1, axis)


def operator(u, e, turned, d):
    mid = e[1] * u[1]
    once = along((u[0] + u[2]) + (u[1] + u[1]), 0)
    twice = along((e[0] * u[0] + e[2] * u[2]) + (mid + mid), 0)
    both = e[1] * once + twice
    sides = roll(turned[0] * once + twice, -1, 1) + roll(turned[1] * once + twice, 1, 1)
    return d * u[1] - (both + both) - sides


def diagonal(e):
    return 64.4 * e[1] + along(along((e[0] + e[2]) + (e[1] + e[1]), 0), 1)


def prepare(j, e, d, turned):
    d[j] = diagonal(e)
    turned[0, j] = roll(e[1], 1, 1)
    turned[1, j] = roll(e[1], -1, 1)


def three(ref, *at):
    *lead, mid = at
    return [ref[(*lead, mid + k)] for k in (-1, 0, 1)]


def total(values):
    return jnp.sum(jnp.sum(values, axis=0, keepdims=True), axis=1, keepdims=True)


def fold(values):
    out = values[0:8]
    for i in range(8, values.shape[0], 8):
        out = out + values[i : i + 8]
    return out


def pick(row, lane, k):
    return jnp.sum(jnp.where(lane == k, row, 0.0), axis=1, keepdims=True)


def on_plane_loop(count, body):
    lax.fori_loop(0, count, lambda i, c: (body(i), c)[1], 0)


def map_kernel(
    ids,
    counts_in,
    *refs,
):
    _map_kernel(ids, counts_in, refs[:7], *refs[7:])


def _map_kernel(
    ids,
    counts_in,
    sources,
    inner,
    outer,
    own,
    pull,
    e_wide,
    history,
    dev,
    extra,
    flat,
    wide,
    counts,
    plastic,
    hard,
    begin,
    delta,
    shear,
    bulk,
    yields,
    count_sem,
    sems,
):
    def copies(z):
        out = []
        for k, (source, target) in enumerate(zip(sources, targets)):
            at = (slice(None), z) if len(source.shape) == 4 else (z,)
            out.append(pltpu.make_async_copy(source.at[at], target.at[at], sems.at[z, k]))
        return out

    targets = (plastic, hard, begin, delta, shear, bulk, yields)
    get_counts = pltpu.make_async_copy(counts_in, counts, count_sem)
    get_counts.start()
    for z in range(DEPTH):
        for copy in copies(z):
            copy.start()
    get_counts.wait()
    group, first = ids[0], ids[1] * BLOCKS
    row = lax.broadcasted_iota(jnp.int32, (FLAT, LANES), 0)

    def plane(z):
        for copy in copies(z):
            copy.wait()
        block = [counts[group, first + 4 * z + b] for b in range(4)]
        turns = jnp.maximum(jnp.maximum(block[0], block[1]), jnp.maximum(block[2], block[3]))
        held = jnp.where(
            row < 2 * BLOCK_ROWS,
            jnp.where(row < BLOCK_ROWS, block[0], block[1]),
            jnp.where(row < 3 * BLOCK_ROWS, block[2], block[3]),
        )
        share = 1.0 / held.astype(F32)
        twice_mu = 2.0 * shear[z]
        elastic = [begin[i, z] - plastic[i, z] for i in range(6)]
        step = [delta[i, z] for i in range(6)]
        third0 = (elastic[0] + elastic[1] + elastic[2]) * (1.0 / 3.0)
        third1 = (step[0] + step[1] + step[2]) * (1.0 / 3.0)
        stress = [twice_mu * (elastic[i] - third0 if i < 3 else elastic[i]) for i in range(6)]
        rate = twice_mu * share
        for i in range(6):
            flat[i] = rate * (step[i] - third1 if i < 3 else step[i])
        floor = root_two_thirds * yields[z]
        limit0 = floor + (root_two_thirds * 0.15) * twice_mu * hard[z]
        most = 1.0 / floor

        def substep(t, carry):
            *s, gone, _, _ = carry
            act = jnp.where(held >= turns - t, 1.0, 0.0)
            s = [s[i] + act * flat[i] for i in range(6)]
            square = s[0] * s[0]
            for i in range(1, 6):
                square = square + s[i] * s[i]
            square = jnp.maximum(square, 1e-30)
            inverse = lax.rsqrt(square)
            over = jnp.maximum(square * inverse - (limit0 + HARDEN * gone), 0.0) * act
            inverse = jnp.minimum(inverse, most)
            theta = 1.0 - (RETURN * over) * inverse
            return (*[theta * s[i] for i in range(6)], gone + over, theta, inverse)

        zero = jnp.zeros((FLAT, LANES), F32)
        *s, gone, theta, inverse = lax.fori_loop(0, turns, substep, (*stress, zero, zero, zero))
        mu = 0.5 * twice_mu
        per = 1.0 / twice_mu
        elastic = [begin[i, z] - plastic[i, z] + delta[i, z] for i in range(6)]
        trace = elastic[0] + elastic[1] + elastic[2]
        third = trace * (1.0 / 3.0)
        for i in range(6):
            whole = elastic[i] - third if i < 3 else elastic[i]
            history[i, z] = plastic[i, z] + (whole - per * s[i])
            dev[i, z] = s[i]
        history[6, z] = hard[z] + (root_two_thirds / 1.1) * per * gone
        pressure = bulk[z] * trace
        ratio = inverse / theta
        coef = mu * theta
        extra[0, z] = pressure
        extra[1, z] = mu * (theta - 1.0) * (ratio * ratio)
        extra[2, z] = coef
        for i in range(6):
            flat[i] = pressure + s[i] if i < 3 else s[i]
        flat[6] = coef * (1.0 / 128.0)
        for i in range(7):
            widen(flat, (i,), wide, (i,))
        e_wide[z] = wide[6]

        def along_x(u):
            return roll(u, -1, 1) - roll(u, 1, 1)

        def along_y(u):
            return roll(u, -1, 0) - roll(u, 1, 0)

        half = 0.5 * half_root
        own[0, z] = 0.5 * along_x(wide[0]) + half * along_y(wide[5])
        own[1, z] = half * along_x(wide[5]) + 0.5 * along_y(wide[1])
        own[2, z] = half * (along_x(wide[4]) + along_y(wide[3]))
        pull[0, z] = half * wide[4]
        pull[1, z] = half * wide[3]
        pull[2, z] = 0.5 * wide[2]

    on_plane_loop(DEPTH, plane)

    for c in range(3):
        own[c, 0] = own[c, 0] + pull[c, 1]
        own[c, 1] = own[c, 1] + pull[c, 2] - pull[c, 0]
        own[c, 2] = own[c, 2] - pull[c, 1]
    facing = 2 - 2 * lax.rem(ids[1], 2)
    for ref, near in ((inner, facing), (outer, 2 - facing)):
        for c in range(3):
            ref[c] = own[c, near]
            ref[3 + c] = own[c, 1]
            ref[6 + c] = pull[c, near]
        ref[9] = e_wide[near]
        ref[10] = e_wide[1]
        ref[11] = e_wide[2 - near]


def sums_kernel(ids, pull_group, pull_block, dev, extra, bulk, history, _, *sends):
    group, slab = ids[0], ids[1]
    lane = lane_of(1)
    pairs = [(i, j) for i in range(6) for j in range(i, 6)]

    def chunk(t, carry):
        z, at = t // 3, pl.multiple_of((t % 3) * 24, 8)
        rows = pl.ds(at, 24)
        s = [dev[i, z, rows] for i in range(6)]
        pressure = extra[0, z, rows]
        weighted = extra[1, z, rows]
        terms = [pressure + s[i] if i < 3 else s[i] for i in range(6)]
        terms += [bulk[z, rows], extra[2, z, rows]]
        ws = [weighted * v for v in s]
        terms += [ws[i] * s[j] for i, j in pairs]
        return tuple(c + fold(v) for c, v in zip(carry, terms))

    zero = jnp.zeros((8, LANES), F32)
    sums = lax.fori_loop(0, 9, chunk, (zero,) * (8 + len(pairs)))
    sums = [total(v) * (1.0 / VOXELS) for v in sums]
    row = jnp.zeros((1, LANES), F32)
    for i in range(6):
        row = jnp.where(lane == i, sums[i], row)
    row = jnp.where(lane == BULK_LANE, sums[6], row)
    row = jnp.where(lane == COEF_LANE, sums[7], row)
    for k, (i, j) in enumerate(pairs):
        hit = (lane == 6 + 6 * i + j) | (lane == 6 + 6 * j + i)
        row = jnp.where(hit, sums[8 + k], row)

    for shift in range(4):
        to = lax.rem(group + shift, 4)
        first = pull_group[to, 2 * slab] == group
        at = jnp.where(first, pull_block[to, 2 * slab], pull_block[to, 2 * slab + 1])
        at = jnp.clip(at - slab * BLOCKS, 0, BLOCKS - 1)
        z, part = at // 4, at % 4
        for b in range(4):

            @pl.when(part == b)
            def _():
                for i in range(7):
                    block = history[i, z, pl.ds(BLOCK_ROWS * b, BLOCK_ROWS)]
                    sends[shift][i, 0:BLOCK_ROWS] = block

        sends[shift][7, 0:1] = row


def inbox_kernel(ids, pull_group, kept, from1, from2, from3, inbox):
    group, slab = ids[0], ids[1]
    sources = (kept, from1, from2, from3)
    for slot in range(2):
        away = lax.rem(group - pull_group[group, 2 * slab + slot] + 4, 4)
        for shift in range(4):

            @pl.when(away == shift)
            def _():
                for i in range(7):
                    inbox[i, pl.ds(slot, BLOCK_ROWS, stride=2)] = sources[shift][i, 0:BLOCK_ROWS]


def sides_of(ids):
    above = 1 - lax.rem(ids[1], 2)
    sign = jnp.where(above == 1, 1.0, -1.0)
    return above, 2 * above, 2 - 2 * above, sign


def outer_kernel(ids, inner, own, pull, message):
    _, facing, _, sign = sides_of(ids)
    for c in range(3):
        message[c] = own[c, facing] + sign * inner[6 + c]
        message[3 + c] = inner[c] - sign * pull[c, facing]
        message[6 + c] = inner[3 + c]
    message[9] = inner[9]
    message[10] = inner[10]


def inner_kernel(ids, outer, own, pull, _0, _1, _2, message):
    _, _, edge, sign = sides_of(ids)
    for c in range(3):
        message[c] = own[c, edge] - sign * outer[6 + c]
        message[3 + c] = outer[c] + sign * pull[c, edge]
        message[6 + c] = outer[3 + c]
    message[9] = outer[9]
    message[10] = outer[10]


def first_kernel(ids, inner, outer, own, pull, e_own, p0, p1, p2, e, moments, d, turned):
    above = 1 - lax.rem(ids[1], 2)
    for c in range(3):
        p0[c, 3] = own[c, 1]
    for z in range(3):
        e[2 + z] = e_own[z]
    for ref, high in ((inner, above), (outer, 1 - above)):
        sign = jnp.where(high == 1, 1.0, -1.0)
        for c in range(3):
            p0[c, 6 * high] = ref[3 + c]
            p0[c, 1 + 4 * high] = ref[c] - sign * pull[c, 2 * high]
            p0[c, 2 + 2 * high] = own[c, 2 * high] + sign * ref[6 + c]
        e[6 * high] = ref[10]
        e[1 + 4 * high] = ref[9]

    for j in range(5):
        ee = three(e, j + 1)
        prepare(j, ee, d, turned)
        sides = (turned[0, j], turned[1, j])
        for c in range(3):
            p1[c, j] = operator(three(p0, c, j + 1), ee, sides, d[j])

    sums = [jnp.zeros((8, LANES), F32)] * 4
    for z in range(3):
        ee = three(e, z + 2)
        sides = (turned[0, z + 1], turned[1, z + 1])
        for c in range(3):
            new = operator(three(p1, c, z + 1), ee, sides, d[z + 1])
            p2[z, c] = new
            r0, r1 = p0[c, z + 2], p1[c, z + 1]
            terms = (r0 * r0, r0 * r1, r1 * r1, r1 * new)
            sums = [a + fold(v) for a, v in zip(sums, terms)]
    lane = lane_of(1)
    keep = lane_of(8) < NVX
    row = jnp.zeros((1, LANES), F32)
    for k in range(4):
        row = jnp.where(lane == k, total(jnp.where(keep, sums[k], 0.0)), row)
    moments[...] = row


def lanczos(m0, m1, m2, m3):
    over = jnp.where(m0 > 0.0, m0, 1.0)
    a0 = jnp.clip(m1 / over, 0.0, 2.1)
    left = jnp.maximum(m2 - 2.0 * a0 * m1 + a0 * a0 * m0, 1e-7 * m2)
    b1 = jnp.clip(left / over, 0.0, 1.2)
    left = jnp.where(left > 0.0, left, 1.0)
    a1 = jnp.clip((m3 - 2.0 * a0 * m2 + a0 * a0 * m1) / left, 0.0, 2.1)
    return a0, a1, b1


class Planes:
    def __init__(self, middle, first, count, far=None, width=0):
        self.middle, self.first, self.count, self.far, self.width = middle, first, count, far, width

    def at(self, k):
        i = k - self.first
        if 0 <= i < self.count:
            return self.middle, i
        return self.far, i + self.width if i < 0 else self.width + i - self.count

    def get(self, k, *lead):
        ref, i = self.at(k)
        return ref[(*lead, i)]

    def set(self, k, value, *lead):
        ref, i = self.at(k)
        ref[(*lead, i)] = value

    def three(self, k, *lead):
        return [self.get(k + i, *lead) for i in (-1, 0, 1)]


def second_kernel(
    ids,
    owner,
    moments,
    kept,
    from1,
    from2,
    from3,
    inner1,
    outer1,
    inner,
    outer,
    p0_in,
    p1_in,
    p2_in,
    e_in,
    d_in,
    turned_in,
    basis,
    gram,
    p0_far,
    p1_far,
    p2_far,
    e_far,
    d_far,
    turned_far,
    v1_all,
    v2_all,
    v3_all,
    v4_all,
):
    p0 = Planes(p0_in, -2, 7, p0_far, 3)
    p1 = Planes(p1_in, -1, 5, p1_far, 3)
    e = Planes(e_in, -2, 7, e_far, 3)
    d = Planes(d_in, -1, 5, d_far, 3)
    turned = Planes(turned_in, -1, 5, turned_far, 3)
    p2 = Planes(None, 0, 3, p2_far, 3)
    v1 = Planes(v1_all, -2, 7)
    v2 = Planes(v2_all, -3, 9)
    v3 = Planes(v3_all, -2, 7)
    v4 = Planes(v4_all, -1, 5)

    lane = lane_of(1)
    found = [pick(moments[...], lane, k) for k in range(4)]
    a0, a1, b1 = lanczos(*found)
    c1, c0 = -(a0 + a1), a0 * a1 - b1
    above = 1 - lax.rem(ids[1], 2)
    for near, ref, high in ((inner1, inner, above), (outer1, outer, 1 - above)):
        for k in range(3):
            place = 2 - k + high * (1 + 2 * k)
            for c in range(3):
                p0_far[c, place] = ref[3 * k + c]
            e_far[place] = near[11] if k == 0 else ref[8 + k]

    far1, far2 = (-4, -3, -2, 4, 5, 6), (-3, -2, -1, 3, 4, 5)
    for k in far1:
        ee = e.three(k)
        d.set(k, diagonal(ee))
        turned.set(k, roll(ee[1], 1, 1), 0)
        turned.set(k, roll(ee[1], -1, 1), 1)

    def apply(field, k, c):
        u = field.three(k, c)
        return u[1], operator(u, e.three(k), (turned.get(k, 0), turned.get(k, 1)), d.get(k))

    for k in far1:
        for c in range(3):
            p1.set(k, apply(p0, k, c)[1], c)
    for k in far2:
        for c in range(3):
            p2.set(k, apply(p1, k, c)[1], c)
    for k in range(-3, 6):
        for c in range(3):
            r0, r1 = p0.get(k, c), p1.get(k, c)
            r2 = p2_in[k, c] if 0 <= k < 3 else p2.get(k, c)
            v2.set(k, r2 + c1 * r1 + c0 * r0, c)
            if -2 <= k <= 4:
                v1.set(k, r1 - a0 * r0, c)
    for k in range(-2, 5):
        for c in range(3):
            mid, new = apply(v2, k, c)
            v3.set(k, new - a1 * mid - b1 * v1.get(k, c), c)
    for k in range(-1, 4):
        for c in range(3):
            mid, new = apply(v3, k, c)
            v4.set(k, new - a1 * mid - b1 * v2.get(k, c), c)

    sums = [jnp.zeros((8, LANES), F32)] * len(PAIRS)
    for z in range(3):
        for c in range(3):
            mid, new = apply(v4, z, c)
            vectors = [p0.get(z, c), v1.get(z, c), v2.get(z, c), v3.get(z, c), mid, new]
            for k in range(5):
                basis[k, c, z] = vectors[k]
            sums = [a + fold(vectors[i] * vectors[j]) for a, (i, j) in zip(sums, PAIRS)]
    keep = lane_of(8) < NVX
    row = jnp.zeros((1, LANES), F32)
    for shift, source in enumerate((kept, from1, from2, from3)):
        mine = owner[lax.rem(ids[0] - shift + 4, 4)] == ids[0]
        row = row + jnp.where(mine, source[7, 0:1], 0.0)
    row = pltpu.roll(jnp.broadcast_to(row, (8, LANES)), SUM_BASE, 1)[0:1]
    sent = [total(jnp.where(keep, v, 0.0)) for v in sums] + [a0, a1, b1] + found
    for k, value in enumerate(sent):
        row = jnp.where(lane == k, value, row)
    gram[...] = jnp.broadcast_to(row, (32, LANES))


def plus(x, y):
    return y if x is None else x if y is None else x + y


def times(x, y):
    if x is None or y is None:
        return None
    return y if isinstance(x, float) else x if isinstance(y, float) else x * y


def inner(g, x, y):
    out = None
    for i in range(6):
        part = None
        for j in range(6):
            part = plus(part, times(g.get((min(i, j), max(i, j))), y[j]))
        out = plus(out, times(x[i], part))
    return out


def minus(x, y):
    return x if y is None else -y if x is None else x - y


def basis_change(own, common):
    a0, a1, b1 = own
    c0, c1, d1 = common
    diag = (a0, a1, a1, a1)
    rows = [[1.0] + [None] * 5, [a0 - c0, 1.0] + [None] * 4]
    for k in range(1, 4):
        last, before, row = rows[k], rows[k - 1], [None] * 6
        for j in range(k + 2):
            value = last[j - 1] if j >= 1 else None
            if j <= 3 and last[j] is not None:
                value = plus(value, times(diag[j] - c1, last[j]))
            if j <= 2:
                value = plus(value, times(b1, last[j + 1]))
            row[j] = minus(value, times(d1, before[j]))
        rows.append(row)
    last, row = rows[4], [None] * 6
    for j in range(5):
        row[j + 1] = plus(row[j + 1], last[j])
        if j <= 3:
            row[j] = plus(row[j], times(diag[j], last[j]))
        if 1 <= j <= 3:
            row[j - 1] = plus(row[j - 1], times(b1, last[j]))
    return rows + [row]


def last_kernel(ids, gram, basis, correction, sums, wide):
    table = gram[...]
    row = jnp.sum(table, axis=0, keepdims=True)
    lane = lane_of(1)
    sides = jnp.concatenate([table, jnp.zeros((LANES - 32, LANES), F32)], axis=0).T
    entry = [sides[k : k + 1] for k in range(len(PAIRS) + 7)]
    own = entry[len(PAIRS) : len(PAIRS) + 3]
    a0, a1, b1 = lanczos(*[jnp.sum(v, axis=1, keepdims=True) for v in entry[len(PAIRS) + 3 :]])
    change = basis_change(own, (a0, a1, b1))
    local = {pair: entry[k] for k, pair in enumerate(PAIRS)}

    def dot(x, y):
        out = None
        for u, v in zip(x, y):
            out = plus(out, times(u, v))
        return out

    half = [[dot(change[k], [local.get((min(j, m), max(j, m))) for j in range(6)]) for m in range(6)] for k in range(5)]
    g = {(k, m): jnp.sum(dot(half[k], change[m]), axis=1, keepdims=True) for k, m in PAIRS}
    one = jnp.ones((1, 1), F32)

    def act(v):
        out = [None] * 6
        diag = (a0, a1, a1, a1, None)
        for i in range(5):
            out[i + 1] = plus(out[i + 1], v[i])
            out[i] = plus(out[i], times(diag[i], v[i]))
            if 1 <= i <= 3:
                out[i - 1] = plus(out[i - 1], times(b1, v[i]))
        return out

    found = [None] * 6
    residual = [one] + [None] * 5
    direction = [one] + [None] * 5
    norm = g[0, 0]
    for turn in range(5):
        image = act(direction)
        alpha = norm / inner(g, direction, image)
        found = [plus(x, times(alpha, v)) for x, v in zip(found, direction)]
        if turn < 4:
            residual = [plus(x, times(-alpha, v)) for x, v in zip(residual, image)]
            new = inner(g, residual, residual)
            beta = new / norm
            direction = [plus(x, times(beta, v)) for x, v in zip(residual, direction)]
            norm = new
    weights = []
    for j in range(5):
        value = jnp.broadcast_to(dot(found[:5], [change[k][j] for k in range(5)]), (1, LANES))
        weights.append(pick(value, lane, ids[1]) * (1.0 / 16.0))

    def plane(z):
        for c in range(3):
            out = weights[0] * basis[0, c, z]
            for k in range(1, 5):
                out = out + weights[k] * basis[k, c, z]
            wide[c] = out
            put(narrow(wide, (c,)), (correction, (c, z)))

    on_plane_loop(DEPTH, plane)

    bulk = pick(row, lane, SUM_BASE + BULK_LANE)
    coef = pick(row, lane, SUM_BASE + COEF_LANE)
    shifted = pltpu.roll(jnp.broadcast_to(row, (8, LANES)), LANES - SUM_BASE, 1)[0:1]
    entry = lane - 6
    i, j = entry // 6, entry % 6
    tangent = (lane >= 6) & (lane < 42)
    normal = tangent & (i < 3) & (j < 3)
    out = jnp.where(tangent, 2.0 * shifted, shifted)
    out = out + jnp.where(tangent & (i == j), 2.0 * coef, 0.0)
    out = out + jnp.where(normal, bulk - (2.0 / 3.0) * coef, 0.0)
    sums[...] = out


def shape(*dims):
    return jax.ShapeDtypeStruct(dims, F32)


def near(*dims):
    return pltpu.VMEM(dims, F32)


def far(*dims):
    return pltpu.HBM(dims, F32)


def in_hbm(array):
    return pltpu.with_memory_space_constraint(array, pltpu.HBM)


VM = pl.BlockSpec(memory_space=pltpu.VMEM)
SM = pl.BlockSpec(memory_space=pltpu.SMEM)
HB = pl.BlockSpec(memory_space=pltpu.HBM)
ANY = pl.BlockSpec(memory_space=pl.ANY)


def call(kernel, in_specs, outs, scratch, args, flops, name, limit=12, out_specs=None):
    size = sum(4 * math.prod(a.shape) for a in (*args, *outs))
    return pl.pallas_call(
        kernel,
        out_shape=tuple(outs),
        in_specs=in_specs,
        out_specs=tuple(out_specs or (VM,) * len(outs)),
        scratch_shapes=[pltpu.VMEM(s, F32) if isinstance(s, tuple) else s for s in scratch],
        compiler_params=pltpu.CompilerParams(vmem_limit_bytes=limit * 2**20),
        cost_estimate=pl.CostEstimate(flops=flops, bytes_accessed=size, transcendentals=0),
        name=name,
    )(*args)


def on_device(
    plastic_strain,
    hardening_var,
    strain_start,
    strain_step,
    shear_mod,
    bulk_mod,
    yield_stress,
    substeps,
    pull_group,
    pull_block,
    owner,
):
    slabs = lax.axis_size("slab")
    ids = jnp.stack([lax.axis_index("rve"), lax.axis_index("slab")]).astype(jnp.int32)
    six = [a.reshape(6, DEPTH, FLAT, LANES) for a in (plastic_strain, strain_start, strain_step)]
    one = [a.reshape(DEPTH, FLAT, LANES) for a in (hardening_var, shear_mod, bulk_mod, yield_stress)]
    plane = (FLAT, LANES)
    wide = (NVX, LANES)

    inner, outer, own, pull, e_own, history, dev, extra = call(
        map_kernel,
        [SM] + [HB] * 8,
        [
            shape(FIRST, *wide),
            shape(FIRST, *wide),
            shape(3, 3, *wide),
            shape(3, 3, *wide),
            shape(3, *wide),
            shape(7, 3, *plane),
            shape(6, 3, *plane),
            shape(3, 3, *plane),
        ],
        [
            pltpu.VMEM((7, *plane), F32),
            pltpu.VMEM((7, *wide), F32),
            pltpu.SMEM((4, 384), jnp.int32),
            pltpu.VMEM((6, DEPTH, *plane), F32),
            pltpu.VMEM((DEPTH, *plane), F32),
            pltpu.VMEM((6, DEPTH, *plane), F32),
            pltpu.VMEM((6, DEPTH, *plane), F32),
            pltpu.VMEM((DEPTH, *plane), F32),
            pltpu.VMEM((DEPTH, *plane), F32),
            pltpu.VMEM((DEPTH, *plane), F32),
            pltpu.SemaphoreType.DMA,
            pltpu.SemaphoreType.DMA((DEPTH, 7)),
        ],
        (ids, *map(in_hbm, (substeps, six[0], one[0], six[1], six[2], one[1], one[2], one[3]))),
        5_000_000,
        "return_map",
    )
    on_chip = [(i, i ^ 1) for i in range(slabs)]
    across = [(i, (i + 1 if i % 2 else i - 1) % slabs) for i in range(slabs)]
    outer1 = lax.ppermute(outer, "slab", across)
    inner1 = lax.ppermute(inner, "slab", on_chip)
    (outer,) = call(
        outer_kernel,
        [SM] + [VM] * 3,
        [shape(SECOND, *wide)],
        [],
        (ids, inner1, own, pull),
        500_000,
        "to_outer",
    )
    outer2 = lax.ppermute(outer, "slab", across)
    kept, *sends = call(
        sums_kernel,
        [SM, SM, SM] + [VM] * 4 + [ANY],
        [shape(8, 24, LANES)] * 4,
        [],
        (ids, pull_group, pull_block, dev, extra, one[2], history, outer),
        2_000_000,
        "element_partials",
    )
    came = [
        lax.ppermute(sends[k - 1], "rve", [(i, (i + k) % 4) for i in range(4)]) for k in (1, 2, 3)
    ]

    (inner,) = call(
        inner_kernel,
        [SM] + [VM] * 3 + [ANY] * 3,
        [shape(SECOND, *wide)],
        [],
        (ids, outer1, own, pull, *came),
        500_000,
        "to_inner",
    )
    inner2 = lax.ppermute(inner, "slab", on_chip)

    p0, p1, p2, e, moments, d, turned = call(
        first_kernel,
        [SM] + [VM] * 5,
        [
            shape(3, 7, *wide),
            shape(3, 5, *wide),
            shape(3, 3, *wide),
            shape(7, *wide),
            shape(1, LANES),
            shape(5, *wide),
            shape(2, 5, *wide),
        ],
        [],
        (ids, inner1, outer1, own, pull, e_own),
        5_000_000,
        "basis_first",
    )
    (inbox,) = call(
        inbox_kernel,
        [SM, SM] + [VM] * 4,
        [shape(7, 2 * BLOCK_ROWS, LANES)],
        [],
        (ids, pull_group, kept, *came),
        100_000,
        "inbox",
    )
    basis, gram = call(
        second_kernel,
        [SM, SM] + [VM] * 15,
        [shape(5, 3, 3, *wide), shape(32, LANES)],
        [
            (3, 6, *wide),
            (3, 6, *wide),
            (3, 6, *wide),
            (6, *wide),
            (6, *wide),
            (2, 6, *wide),
            (3, 7, *wide),
            (3, 9, *wide),
            (3, 7, *wide),
            (3, 5, *wide),
        ],
        (ids, owner, moments, kept, *came, inner1, outer1, inner2, outer2, p0, p1, p2, e, d, turned),
        12_000_000,
        "basis_second",
    )
    gram = lax.all_to_all(gram, "slab", split_axis=0, concat_axis=0, tiled=True)
    correction, element = call(
        last_kernel,
        [SM, VM, VM],
        [shape(3, 3, *plane), shape(1, LANES)],
        [(3, *wide)],
        (ids, gram, basis),
        1_000_000,
        "combine",
    )
    inbox = inbox.reshape(7, BLOCK_ROWS, 2, LANES).transpose(0, 2, 1, 3)
    return (
        correction.reshape(3, 1, DEPTH, FLAT * LANES),
        inbox.reshape(7, 1, 2, BLOCK_ROWS * LANES),
        element[:, :42],
    )


def solution(mesh):
    return jax.shard_map(
        on_device,
        mesh=mesh,
        in_specs=(
            P(None, "rve", "slab", None),
            P("rve", "slab", None),
            P(None, "rve", "slab", None),
            P(None, "rve", "slab", None),
            P("rve", "slab", None),
            P("rve", "slab", None),
            P("rve", "slab", None),
            P(),
            P(),
            P(),
            P(),
        ),
        out_specs=(P(None, "rve", "slab", None), P(None, "rve", "slab", None), P("rve", None)),
        check_vma=False,
    )
```

```python
import math

import jax
import jax.numpy as jnp
from jax import lax
from jax.experimental import pallas as pl
from jax.experimental.pallas import tpu as pltpu
from jax.sharding import PartitionSpec as P

NVX = 96
LANES = 128
FLAT = 72
DEPTH = 3
BLOCK_ROWS = 18
BLOCKS = 12
VOXELS = 884736.0
F32 = jnp.float32

root_two_thirds = math.sqrt(2.0 / 3.0)
half_root = 1.0 / math.sqrt(2.0)
RETURN = 2.0 / 2.2
HARDEN = 0.2 / 2.2

BULK_LANE = 42
COEF_LANE = 43
SUM_BASE = 64
PAIRS = [(i, j) for i in range(6) for j in range(i, 6) if (i, j) != (5, 5)]

FIRST = 12
SECOND = 11


def roll(values, shift, axis):
    return pltpu.roll(values, shift % values.shape[axis], axis)


def lane_of(rows):
    return lax.broadcasted_iota(jnp.int32, (rows, LANES), 1)


def widen(flat_ref, at, wide_ref, to):
    lane = lane_of(24)
    x = jnp.where(lane < 96, lane, jnp.where(lane < 112, lane - 96, lane - 32))
    a = [flat_ref[(*at, pl.ds(i, 24, stride=3), slice(None))] for i in range(3)]

    def take(i, place):
        return jnp.take_along_axis(a[i], place & 127, axis=1, mode="promise_in_bounds")

    second, third, last = 96 + x, 192 + x, 288 + x
    rows = [
        take(0, x),
        jnp.where(second < 128, take(0, second), take(1, second)),
        jnp.where(third < 256, take(1, third), take(2, third)),
        take(2, last),
    ]
    for i, row in enumerate(rows):
        wide_ref[(*to, pl.ds(i, 24, stride=4), slice(None))] = row


def narrow(wide_ref, at):
    lane = lane_of(24)
    o0, o1, o2, o3 = [wide_ref[(*at, pl.ds(i, 24, stride=4), slice(None))] for i in range(4)]
    r1, r2, r3 = roll(o1, 96, 1), roll(o2, 64, 1), roll(o3, 32, 1)
    return (
        jnp.where(lane < 96, o0, r1),
        jnp.where(lane < 64, r1, r2),
        jnp.where(lane < 32, r2, r3),
    )


def put(rows, *targets):
    for ref, to in targets:
        for i in range(3):
            ref[(*to, pl.ds(i, 24, stride=3), slice(None))] = rows[i]


def along(values, axis):
    values = values + roll(values, 1, axis)
    return values + roll(values, -1, axis)


def operator(u, e, turned, d):
    mid = e[1] * u[1]
    once = along((u[0] + u[2]) + (u[1] + u[1]), 0)
    twice = along((e[0] * u[0] + e[2] * u[2]) + (mid + mid), 0)
    both = e[1] * once + twice
    sides = roll(turned[0] * once + twice, -1, 1) + roll(turned[1] * once + twice, 1, 1)
    return d * u[1] - (both + both) - sides


def diagonal(e):
    return 64.4 * e[1] + along(along((e[0] + e[2]) + (e[1] + e[1]), 0), 1)


def prepare(j, e, d, turned):
    d[j] = diagonal(e)
    turned[0, j] = roll(e[1], 1, 1)
    turned[1, j] = roll(e[1], -1, 1)


def three(ref, *at):
    *lead, mid = at
    return [ref[(*lead, mid + k)] for k in (-1, 0, 1)]


def total(values):
    return jnp.sum(jnp.sum(values, axis=0, keepdims=True), axis=1, keepdims=True)


def fold(values):
    out = values[0:8]
    for i in range(8, values.shape[0], 8):
        out = out + values[i : i + 8]
    return out


def pick(row, lane, k):
    return jnp.sum(jnp.where(lane == k, row, 0.0), axis=1, keepdims=True)


def on_plane_loop(count, body):
    lax.fori_loop(0, count, lambda i, c: (body(i), c)[1], 0)


def map_kernel(
    ids,
    counts_in,
    *refs,
):
    _map_kernel(ids, counts_in, refs[:7], *refs[7:])


def _map_kernel(
    ids,
    counts_in,
    sources,
    inner,
    outer,
    own,
    pull,
    e_wide,
    history,
    dev,
    extra,
    flat,
    wide,
    counts,
    plastic,
    hard,
    begin,
    delta,
    shear,
    bulk,
    yields,
    count_sem,
    sems,
):
    def copies(z):
        out = []
        for k, (source, target) in enumerate(zip(sources, targets)):
            at = (slice(None), z) if len(source.shape) == 4 else (z,)
            out.append(pltpu.make_async_copy(source.at[at], target.at[at], sems.at[z, k]))
        return out

    targets = (plastic, hard, begin, delta, shear, bulk, yields)
    get_counts = pltpu.make_async_copy(counts_in, counts, count_sem)
    get_counts.start()
    for z in range(DEPTH):
        for copy in copies(z):
            copy.start()
    get_counts.wait()
    group, first = ids[0], ids[1] * BLOCKS
    row = lax.broadcasted_iota(jnp.int32, (FLAT, LANES), 0)

    def plane(z):
        for copy in copies(z):
            copy.wait()
        block = [counts[group, first + 4 * z + b] for b in range(4)]
        turns = jnp.maximum(jnp.maximum(block[0], block[1]), jnp.maximum(block[2], block[3]))
        held = jnp.where(
            row < 2 * BLOCK_ROWS,
            jnp.where(row < BLOCK_ROWS, block[0], block[1]),
            jnp.where(row < 3 * BLOCK_ROWS, block[2], block[3]),
        )
        share = 1.0 / held.astype(F32)
        twice_mu = 2.0 * shear[z]
        elastic = [begin[i, z] - plastic[i, z] for i in range(6)]
        step = [delta[i, z] for i in range(6)]
        third0 = (elastic[0] + elastic[1] + elastic[2]) * (1.0 / 3.0)
        third1 = (step[0] + step[1] + step[2]) * (1.0 / 3.0)
        stress = [twice_mu * (elastic[i] - third0 if i < 3 else elastic[i]) for i in range(6)]
        rate = twice_mu * share
        for i in range(6):
            flat[i] = rate * (step[i] - third1 if i < 3 else step[i])
        floor = root_two_thirds * yields[z]
        limit0 = floor + (root_two_thirds * 0.15) * twice_mu * hard[z]
        most = 1.0 / floor

        def substep(t, carry):
            *s, gone, _, _ = carry
            act = jnp.where(held >= turns - t, 1.0, 0.0)
            s = [s[i] + act * flat[i] for i in range(6)]
            square = s[0] * s[0]
            for i in range(1, 6):
                square = square + s[i] * s[i]
            square = jnp.maximum(square, 1e-30)
            inverse = lax.rsqrt(square)
            over = jnp.maximum(square * inverse - (limit0 + HARDEN * gone), 0.0) * act
            inverse = jnp.minimum(inverse, most)
            theta = 1.0 - (RETURN * over) * inverse
            return (*[theta * s[i] for i in range(6)], gone + over, theta, inverse)

        zero = jnp.zeros((FLAT, LANES), F32)
        *s, gone, theta, inverse = lax.fori_loop(0, turns, substep, (*stress, zero, zero, zero))
        mu = 0.5 * twice_mu
        per = 1.0 / twice_mu
        elastic = [begin[i, z] - plastic[i, z] + delta[i, z] for i in range(6)]
        trace = elastic[0] + elastic[1] + elastic[2]
        third = trace * (1.0 / 3.0)
        for i in range(6):
            whole = elastic[i] - third if i < 3 else elastic[i]
            history[i, z] = plastic[i, z] + (whole - per * s[i])
            dev[i, z] = s[i]
        history[6, z] = hard[z] + (root_two_thirds / 1.1) * per * gone
        pressure = bulk[z] * trace
        ratio = inverse / theta
        coef = mu * theta
        extra[0, z] = pressure
        extra[1, z] = mu * (theta - 1.0) * (ratio * ratio)
        extra[2, z] = coef
        for i in range(6):
            flat[i] = pressure + s[i] if i < 3 else s[i]
        flat[6] = coef * (1.0 / 128.0)
        for i in range(7):
            widen(flat, (i,), wide, (i,))
        e_wide[z] = wide[6]

        def along_x(u):
            return roll(u, -1, 1) - roll(u, 1, 1)

        def along_y(u):
            return roll(u, -1, 0) - roll(u, 1, 0)

        half = 0.5 * half_root
        own[0, z] = 0.5 * along_x(wide[0]) + half * along_y(wide[5])
        own[1, z] = half * along_x(wide[5]) + 0.5 * along_y(wide[1])
        own[2, z] = half * (along_x(wide[4]) + along_y(wide[3]))
        pull[0, z] = half * wide[4]
        pull[1, z] = half * wide[3]
        pull[2, z] = 0.5 * wide[2]

    on_plane_loop(DEPTH, plane)

    for c in range(3):
        own[c, 0] = own[c, 0] + pull[c, 1]
        own[c, 1] = own[c, 1] + pull[c, 2] - pull[c, 0]
        own[c, 2] = own[c, 2] - pull[c, 1]
    facing = 2 - 2 * lax.rem(ids[1], 2)
    for ref, near in ((inner, facing), (outer, 2 - facing)):
        for c in range(3):
            ref[c] = own[c, near]
            ref[3 + c] = own[c, 1]
            ref[6 + c] = pull[c, near]
        ref[9] = e_wide[near]
        ref[10] = e_wide[1]
        ref[11] = e_wide[2 - near]


def sums_kernel(ids, pull_group, pull_block, dev, extra, bulk, history, _, *sends):
    group, slab = ids[0], ids[1]
    lane = lane_of(1)
    pairs = [(i, j) for i in range(6) for j in range(i, 6)]

    def chunk(t, carry):
        z, at = t // 3, pl.multiple_of((t % 3) * 24, 8)
        rows = pl.ds(at, 24)
        s = [dev[i, z, rows] for i in range(6)]
        pressure = extra[0, z, rows]
        weighted = extra[1, z, rows]
        terms = [pressure + s[i] if i < 3 else s[i] for i in range(6)]
        terms += [bulk[z, rows], extra[2, z, rows]]
        ws = [weighted * v for v in s]
        terms += [ws[i] * s[j] for i, j in pairs]
        return tuple(c + fold(v) for c, v in zip(carry, terms))

    zero = jnp.zeros((8, LANES), F32)
    sums = lax.fori_loop(0, 9, chunk, (zero,) * (8 + len(pairs)))
    sums = [total(v) * (1.0 / VOXELS) for v in sums]
    row = jnp.zeros((1, LANES), F32)
    for i in range(6):
        row = jnp.where(lane == i, sums[i], row)
    row = jnp.where(lane == BULK_LANE, sums[6], row)
    row = jnp.where(lane == COEF_LANE, sums[7], row)
    for k, (i, j) in enumerate(pairs):
        hit = (lane == 6 + 6 * i + j) | (lane == 6 + 6 * j + i)
        row = jnp.where(hit, sums[8 + k], row)

    for shift in range(4):
        to = lax.rem(group + shift, 4)
        first = pull_group[to, 2 * slab] == group
        at = jnp.where(first, pull_block[to, 2 * slab], pull_block[to, 2 * slab + 1])
        at = jnp.clip(at - slab * BLOCKS, 0, BLOCKS - 1)
        z, part = at // 4, at % 4
        for b in range(4):

            @pl.when(part == b)
            def _():
                for i in range(7):
                    block = history[i, z, pl.ds(BLOCK_ROWS * b, BLOCK_ROWS)]
                    sends[shift][i, 0:BLOCK_ROWS] = block

        sends[shift][7, 0:1] = row


def rows_kernel(ids, owner, kept, from1, from2, from3, summed):
    row = jnp.zeros((1, LANES), F32)
    for shift, source in enumerate((kept, from1, from2, from3)):
        mine = owner[lax.rem(ids[0] - shift + 4, 4)] == ids[0]
        row = row + jnp.where(mine, source[7, 0:1], 0.0)
    summed[...] = row


def inbox_kernel(ids, pull_group, kept, from1, from2, from3, _, inbox):
    group, slab = ids[0], ids[1]
    sources = (kept, from1, from2, from3)
    for slot in range(2):
        away = lax.rem(group - pull_group[group, 2 * slab + slot] + 4, 4)
        for shift in range(4):

            @pl.when(away == shift)
            def _():
                for i in range(7):
                    inbox[i, pl.ds(slot, BLOCK_ROWS, stride=2)] = sources[shift][i, 0:BLOCK_ROWS]


def sides_of(ids):
    above = 1 - lax.rem(ids[1], 2)
    sign = jnp.where(above == 1, 1.0, -1.0)
    return above, 2 * above, 2 - 2 * above, sign


def outer_kernel(ids, inner, own, pull, message):
    _, facing, _, sign = sides_of(ids)
    for c in range(3):
        message[c] = own[c, facing] + sign * inner[6 + c]
        message[3 + c] = inner[c] - sign * pull[c, facing]
        message[6 + c] = inner[3 + c]
    message[9] = inner[9]
    message[10] = inner[10]


def inner_kernel(ids, outer, own, pull, _0, _1, message):
    _, _, edge, sign = sides_of(ids)
    for c in range(3):
        message[c] = own[c, edge] - sign * outer[6 + c]
        message[3 + c] = outer[c] + sign * pull[c, edge]
        message[6 + c] = outer[3 + c]
    message[9] = outer[9]
    message[10] = outer[10]


def first_kernel(ids, inner, outer, own, pull, e_own, p0, p1, p2, e, moments, d, turned):
    above = 1 - lax.rem(ids[1], 2)
    for c in range(3):
        p0[c, 3] = own[c, 1]
    for z in range(3):
        e[2 + z] = e_own[z]
    for ref, high in ((inner, above), (outer, 1 - above)):
        sign = jnp.where(high == 1, 1.0, -1.0)
        for c in range(3):
            p0[c, 6 * high] = ref[3 + c]
            p0[c, 1 + 4 * high] = ref[c] - sign * pull[c, 2 * high]
            p0[c, 2 + 2 * high] = own[c, 2 * high] + sign * ref[6 + c]
        e[6 * high] = ref[10]
        e[1 + 4 * high] = ref[9]

    for j in range(5):
        ee = three(e, j + 1)
        prepare(j, ee, d, turned)
        sides = (turned[0, j], turned[1, j])
        for c in range(3):
            p1[c, j] = operator(three(p0, c, j + 1), ee, sides, d[j])

    sums = [jnp.zeros((8, LANES), F32)] * 4
    for z in range(3):
        ee = three(e, z + 2)
        sides = (turned[0, z + 1], turned[1, z + 1])
        for c in range(3):
            new = operator(three(p1, c, z + 1), ee, sides, d[z + 1])
            p2[z, c] = new
            r0, r1 = p0[c, z + 2], p1[c, z + 1]
            terms = (r0 * r0, r0 * r1, r1 * r1, r1 * new)
            sums = [a + fold(v) for a, v in zip(sums, terms)]
    lane = lane_of(1)
    keep = lane_of(8) < NVX
    row = jnp.zeros((1, LANES), F32)
    for k in range(4):
        row = jnp.where(lane == k, total(jnp.where(keep, sums[k], 0.0)), row)
    moments[...] = row


def lanczos(m0, m1, m2, m3):
    over = jnp.where(m0 > 0.0, m0, 1.0)
    a0 = jnp.clip(m1 / over, 0.0, 2.1)
    left = jnp.maximum(m2 - 2.0 * a0 * m1 + a0 * a0 * m0, 1e-7 * m2)
    b1 = jnp.clip(left / over, 0.0, 1.2)
    left = jnp.where(left > 0.0, left, 1.0)
    a1 = jnp.clip((m3 - 2.0 * a0 * m2 + a0 * a0 * m1) / left, 0.0, 2.1)
    return a0, a1, b1


class Planes:
    def __init__(self, middle, first, count, far=None, width=0):
        self.middle, self.first, self.count, self.far, self.width = middle, first, count, far, width

    def at(self, k):
        i = k - self.first
        if 0 <= i < self.count:
            return self.middle, i
        return self.far, i + self.width if i < 0 else self.width + i - self.count

    def get(self, k, *lead):
        ref, i = self.at(k)
        return ref[(*lead, i)]

    def set(self, k, value, *lead):
        ref, i = self.at(k)
        ref[(*lead, i)] = value

    def three(self, k, *lead):
        return [self.get(k + i, *lead) for i in (-1, 0, 1)]


def second_kernel(
    ids,
    moments,
    summed,
    inner1,
    outer1,
    inner,
    outer,
    p0_in,
    p1_in,
    p2_in,
    e_in,
    d_in,
    turned_in,
    basis,
    gram,
    p0_far,
    p1_far,
    p2_far,
    e_far,
    d_far,
    turned_far,
    v1_all,
    v2_all,
    v3_all,
    v4_all,
):
    p0 = Planes(p0_in, -2, 7, p0_far, 3)
    p1 = Planes(p1_in, -1, 5, p1_far, 3)
    e = Planes(e_in, -2, 7, e_far, 3)
    d = Planes(d_in, -1, 5, d_far, 3)
    turned = Planes(turned_in, -1, 5, turned_far, 3)
    p2 = Planes(None, 0, 3, p2_far, 3)
    v1 = Planes(v1_all, -2, 7)
    v2 = Planes(v2_all, -3, 9)
    v3 = Planes(v3_all, -2, 7)
    v4 = Planes(v4_all, -1, 5)

    lane = lane_of(1)
    found = [pick(moments[...], lane, k) for k in range(4)]
    a0, a1, b1 = lanczos(*found)
    c1, c0 = -(a0 + a1), a0 * a1 - b1
    above = 1 - lax.rem(ids[1], 2)
    for near, ref, high in ((inner1, inner, above), (outer1, outer, 1 - above)):
        for k in range(3):
            place = 2 - k + high * (1 + 2 * k)
            for c in range(3):
                p0_far[c, place] = ref[3 * k + c]
            e_far[place] = near[11] if k == 0 else ref[8 + k]

    far1, far2 = (-4, -3, -2, 4, 5, 6), (-3, -2, -1, 3, 4, 5)
    for k in far1:
        ee = e.three(k)
        d.set(k, diagonal(ee))
        turned.set(k, roll(ee[1], 1, 1), 0)
        turned.set(k, roll(ee[1], -1, 1), 1)

    def apply(field, k, c):
        u = field.three(k, c)
        return u[1], operator(u, e.three(k), (turned.get(k, 0), turned.get(k, 1)), d.get(k))

    for k in far1:
        for c in range(3):
            p1.set(k, apply(p0, k, c)[1], c)
    for k in far2:
        for c in range(3):
            p2.set(k, apply(p1, k, c)[1], c)
    for k in range(-3, 6):
        for c in range(3):
            r0, r1 = p0.get(k, c), p1.get(k, c)
            r2 = p2_in[k, c] if 0 <= k < 3 else p2.get(k, c)
            v2.set(k, r2 + c1 * r1 + c0 * r0, c)
            if -2 <= k <= 4:
                v1.set(k, r1 - a0 * r0, c)
    for k in range(-2, 5):
        for c in range(3):
            mid, new = apply(v2, k, c)
            v3.set(k, new - a1 * mid - b1 * v1.get(k, c), c)
    for k in range(-1, 4):
        for c in range(3):
            mid, new = apply(v3, k, c)
            v4.set(k, new - a1 * mid - b1 * v2.get(k, c), c)

    sums = [jnp.zeros((8, LANES), F32)] * len(PAIRS)
    for z in range(3):
        for c in range(3):
            mid, new = apply(v4, z, c)
            vectors = [p0.get(z, c), v1.get(z, c), v2.get(z, c), v3.get(z, c), mid, new]
            for k in range(5):
                basis[k, c, z] = vectors[k]
            sums = [a + fold(vectors[i] * vectors[j]) for a, (i, j) in zip(sums, PAIRS)]
    keep = lane_of(8) < NVX
    row = pltpu.roll(jnp.broadcast_to(summed[...], (8, LANES)), SUM_BASE, 1)[0:1]
    sent = [total(jnp.where(keep, v, 0.0)) for v in sums] + [a0, a1, b1] + found
    for k, value in enumerate(sent):
        row = jnp.where(lane == k, value, row)
    gram[...] = jnp.broadcast_to(row, (32, LANES))


def plus(x, y):
    return y if x is None else x if y is None else x + y


def times(x, y):
    if x is None or y is None:
        return None
    return y if isinstance(x, float) else x if isinstance(y, float) else x * y


def inner(g, x, y):
    out = None
    for i in range(6):
        part = None
        for j in range(6):
            part = plus(part, times(g.get((min(i, j), max(i, j))), y[j]))
        out = plus(out, times(x[i], part))
    return out


def minus(x, y):
    return x if y is None else -y if x is None else x - y


def basis_change(own, common):
    a0, a1, b1 = own
    c0, c1, d1 = common
    diag = (a0, a1, a1, a1)
    rows = [[1.0] + [None] * 5, [a0 - c0, 1.0] + [None] * 4]
    for k in range(1, 4):
        last, before, row = rows[k], rows[k - 1], [None] * 6
        for j in range(k + 2):
            value = last[j - 1] if j >= 1 else None
            if j <= 3 and last[j] is not None:
                value = plus(value, times(diag[j] - c1, last[j]))
            if j <= 2:
                value = plus(value, times(b1, last[j + 1]))
            row[j] = minus(value, times(d1, before[j]))
        rows.append(row)
    last, row = rows[4], [None] * 6
    for j in range(5):
        row[j + 1] = plus(row[j + 1], last[j])
        if j <= 3:
            row[j] = plus(row[j], times(diag[j], last[j]))
        if 1 <= j <= 3:
            row[j - 1] = plus(row[j - 1], times(b1, last[j]))
    return rows + [row]


def last_kernel(ids, gram, basis, correction, sums, wide):
    table = gram[...]
    row = jnp.sum(table, axis=0, keepdims=True)
    lane = lane_of(1)
    sides = jnp.concatenate([table, jnp.zeros((LANES - 32, LANES), F32)], axis=0).T
    entry = [sides[k : k + 1] for k in range(len(PAIRS) + 7)]
    own = entry[len(PAIRS) : len(PAIRS) + 3]
    a0, a1, b1 = lanczos(*[jnp.sum(v, axis=1, keepdims=True) for v in entry[len(PAIRS) + 3 :]])
    change = basis_change(own, (a0, a1, b1))
    local = {pair: entry[k] for k, pair in enumerate(PAIRS)}

    def dot(x, y):
        out = None
        for u, v in zip(x, y):
            out = plus(out, times(u, v))
        return out

    half = [[dot(change[k], [local.get((min(j, m), max(j, m))) for j in range(6)]) for m in range(6)] for k in range(5)]
    g = {(k, m): jnp.sum(dot(half[k], change[m]), axis=1, keepdims=True) for k, m in PAIRS}
    one = jnp.ones((1, 1), F32)

    def act(v):
        out = [None] * 6
        diag = (a0, a1, a1, a1, None)
        for i in range(5):
            out[i + 1] = plus(out[i + 1], v[i])
            out[i] = plus(out[i], times(diag[i], v[i]))
            if 1 <= i <= 3:
                out[i - 1] = plus(out[i - 1], times(b1, v[i]))
        return out

    found = [None] * 6
    residual = [one] + [None] * 5
    direction = [one] + [None] * 5
    norm = g[0, 0]
    for turn in range(5):
        image = act(direction)
        alpha = norm / inner(g, direction, image)
        found = [plus(x, times(alpha, v)) for x, v in zip(found, direction)]
        if turn < 4:
            residual = [plus(x, times(-alpha, v)) for x, v in zip(residual, image)]
            new = inner(g, residual, residual)
            beta = new / norm
            direction = [plus(x, times(beta, v)) for x, v in zip(residual, direction)]
            norm = new
    weights = []
    for j in range(5):
        value = jnp.broadcast_to(dot(found[:5], [change[k][j] for k in range(5)]), (1, LANES))
        weights.append(pick(value, lane, ids[1]) * (1.0 / 16.0))

    def plane(z):
        for c in range(3):
            out = weights[0] * basis[0, c, z]
            for k in range(1, 5):
                out = out + weights[k] * basis[k, c, z]
            wide[c] = out
            put(narrow(wide, (c,)), (correction, (c, z)))

    on_plane_loop(DEPTH, plane)

    bulk = pick(row, lane, SUM_BASE + BULK_LANE)
    coef = pick(row, lane, SUM_BASE + COEF_LANE)
    shifted = pltpu.roll(jnp.broadcast_to(row, (8, LANES)), LANES - SUM_BASE, 1)[0:1]
    entry = lane - 6
    i, j = entry // 6, entry % 6
    tangent = (lane >= 6) & (lane < 42)
    normal = tangent & (i < 3) & (j < 3)
    out = jnp.where(tangent, 2.0 * shifted, shifted)
    out = out + jnp.where(tangent & (i == j), 2.0 * coef, 0.0)
    out = out + jnp.where(normal, bulk - (2.0 / 3.0) * coef, 0.0)
    sums[...] = out


def shape(*dims):
    return jax.ShapeDtypeStruct(dims, F32)


def near(*dims):
    return pltpu.VMEM(dims, F32)


def far(*dims):
    return pltpu.HBM(dims, F32)


def in_hbm(array):
    return pltpu.with_memory_space_constraint(array, pltpu.HBM)


VM = pl.BlockSpec(memory_space=pltpu.VMEM)
SM = pl.BlockSpec(memory_space=pltpu.SMEM)
HB = pl.BlockSpec(memory_space=pltpu.HBM)
ANY = pl.BlockSpec(memory_space=pl.ANY)


def call(kernel, in_specs, outs, scratch, args, flops, name, limit=12, out_specs=None):
    size = sum(4 * math.prod(a.shape) for a in (*args, *outs))
    return pl.pallas_call(
        kernel,
        out_shape=tuple(outs),
        in_specs=in_specs,
        out_specs=tuple(out_specs or (VM,) * len(outs)),
        scratch_shapes=[pltpu.VMEM(s, F32) if isinstance(s, tuple) else s for s in scratch],
        compiler_params=pltpu.CompilerParams(vmem_limit_bytes=limit * 2**20),
        cost_estimate=pl.CostEstimate(flops=flops, bytes_accessed=size, transcendentals=0),
        name=name,
    )(*args)


def on_device(
    plastic_strain,
    hardening_var,
    strain_start,
    strain_step,
    shear_mod,
    bulk_mod,
    yield_stress,
    substeps,
    pull_group,
    pull_block,
    owner,
):
    slabs = lax.axis_size("slab")
    ids = jnp.stack([lax.axis_index("rve"), lax.axis_index("slab")]).astype(jnp.int32)
    six = [a.reshape(6, DEPTH, FLAT, LANES) for a in (plastic_strain, strain_start, strain_step)]
    one = [a.reshape(DEPTH, FLAT, LANES) for a in (hardening_var, shear_mod, bulk_mod, yield_stress)]
    plane = (FLAT, LANES)
    wide = (NVX, LANES)

    inner, outer, own, pull, e_own, history, dev, extra = call(
        map_kernel,
        [SM] + [HB] * 8,
        [
            shape(FIRST, *wide),
            shape(FIRST, *wide),
            shape(3, 3, *wide),
            shape(3, 3, *wide),
            shape(3, *wide),
            shape(7, 3, *plane),
            shape(6, 3, *plane),
            shape(3, 3, *plane),
        ],
        [
            pltpu.VMEM((7, *plane), F32),
            pltpu.VMEM((7, *wide), F32),
            pltpu.SMEM((4, 384), jnp.int32),
            pltpu.VMEM((6, DEPTH, *plane), F32),
            pltpu.VMEM((DEPTH, *plane), F32),
            pltpu.VMEM((6, DEPTH, *plane), F32),
            pltpu.VMEM((6, DEPTH, *plane), F32),
            pltpu.VMEM((DEPTH, *plane), F32),
            pltpu.VMEM((DEPTH, *plane), F32),
            pltpu.VMEM((DEPTH, *plane), F32),
            pltpu.SemaphoreType.DMA,
            pltpu.SemaphoreType.DMA((DEPTH, 7)),
        ],
        (ids, *map(in_hbm, (substeps, six[0], one[0], six[1], six[2], one[1], one[2], one[3]))),
        5_000_000,
        "return_map",
    )
    on_chip = [(i, i ^ 1) for i in range(slabs)]
    across = [(i, (i + 1 if i % 2 else i - 1) % slabs) for i in range(slabs)]
    outer1 = lax.ppermute(outer, "slab", across)
    inner1 = lax.ppermute(inner, "slab", on_chip)
    (outer,) = call(
        outer_kernel,
        [SM] + [VM] * 3,
        [shape(SECOND, *wide)],
        [],
        (ids, inner1, own, pull),
        500_000,
        "to_outer",
    )
    outer2 = lax.ppermute(outer, "slab", across)
    kept, *sends = call(
        sums_kernel,
        [SM, SM, SM] + [VM] * 4 + [ANY],
        [shape(8, 24, LANES)] * 4,
        [],
        (ids, pull_group, pull_block, dev, extra, one[2], history, outer),
        2_000_000,
        "element_partials",
    )
    came = [
        lax.ppermute(sends[k - 1], "rve", [(i, (i + k) % 4) for i in range(4)]) for k in (1, 2, 3)
    ]

    (inner,) = call(
        inner_kernel,
        [SM] + [VM] * 3 + [ANY] * 2,
        [shape(SECOND, *wide)],
        [],
        (ids, outer1, own, pull, kept, came[1]),
        500_000,
        "to_inner",
    )
    inner2 = lax.ppermute(inner, "slab", on_chip)

    p0, p1, p2, e, moments, d, turned = call(
        first_kernel,
        [SM] + [VM] * 5,
        [
            shape(3, 7, *wide),
            shape(3, 5, *wide),
            shape(3, 3, *wide),
            shape(7, *wide),
            shape(1, LANES),
            shape(5, *wide),
            shape(2, 5, *wide),
        ],
        [],
        (ids, inner1, outer1, own, pull, e_own),
        5_000_000,
        "basis_first",
    )
    (summed,) = call(
        rows_kernel,
        [SM, SM] + [VM] * 4,
        [shape(1, LANES)],
        [],
        (ids, owner, kept, *came),
        100_000,
        "rows",
    )
    basis, gram = call(
        second_kernel,
        [SM] + [VM] * 12,
        [shape(5, 3, 3, *wide), shape(32, LANES)],
        [
            (3, 6, *wide),
            (3, 6, *wide),
            (3, 6, *wide),
            (6, *wide),
            (6, *wide),
            (2, 6, *wide),
            (3, 7, *wide),
            (3, 9, *wide),
            (3, 7, *wide),
            (3, 5, *wide),
        ],
        (ids, moments, summed, inner1, outer1, inner2, outer2, p0, p1, p2, e, d, turned),
        12_000_000,
        "basis_second",
    )
    (inbox,) = call(
        inbox_kernel,
        [SM, SM] + [VM] * 4 + [ANY],
        [shape(7, 2 * BLOCK_ROWS, LANES)],
        [],
        (ids, pull_group, kept, *came, basis),
        100_000,
        "inbox",
    )
    gram = lax.all_to_all(gram, "slab", split_axis=0, concat_axis=0, tiled=True)
    correction, element = call(
        last_kernel,
        [SM, VM, VM],
        [shape(3, 3, *plane), shape(1, LANES)],
        [(3, *wide)],
        (ids, gram, basis),
        1_000_000,
        "combine",
    )
    inbox = inbox.reshape(7, BLOCK_ROWS, 2, LANES).transpose(0, 2, 1, 3)
    return (
        correction.reshape(3, 1, DEPTH, FLAT * LANES),
        inbox.reshape(7, 1, 2, BLOCK_ROWS * LANES),
        element[:, :42],
    )


def solution(mesh):
    return jax.shard_map(
        on_device,
        mesh=mesh,
        in_specs=(
            P(None, "rve", "slab", None),
            P("rve", "slab", None),
            P(None, "rve", "slab", None),
            P(None, "rve", "slab", None),
            P("rve", "slab", None),
            P("rve", "slab", None),
            P("rve", "slab", None),
            P(),
            P(),
            P(),
            P(),
        ),
        out_specs=(P(None, "rve", "slab", None), P(None, "rve", "slab", None), P("rve", None)),
        check_vma=False,
    )
```

```python
import math

import jax
import jax.numpy as jnp
from jax import lax
from jax.experimental import pallas as pl
from jax.experimental.pallas import tpu as pltpu
from jax.sharding import PartitionSpec as P

NVX = 96
LANES = 128
FLAT = 72
DEPTH = 3
BLOCK_ROWS = 18
BLOCKS = 12
VOXELS = 884736.0
F32 = jnp.float32

root_two_thirds = math.sqrt(2.0 / 3.0)
half_root = 1.0 / math.sqrt(2.0)
RETURN = 2.0 / 2.2
HARDEN = 0.2 / 2.2

BULK_LANE = 42
COEF_LANE = 43
SUM_BASE = 64
PAIRS = [(i, j) for i in range(6) for j in range(i, 6) if (i, j) != (5, 5)]

FIRST = 12
SECOND = 11


def roll(values, shift, axis):
    return pltpu.roll(values, shift % values.shape[axis], axis)


def lane_of(rows):
    return lax.broadcasted_iota(jnp.int32, (rows, LANES), 1)


def widen(flat_ref, at, wide_ref, to):
    lane = lane_of(24)
    x = jnp.where(lane < 96, lane, jnp.where(lane < 112, lane - 96, lane - 32))
    a = [flat_ref[(*at, pl.ds(i, 24, stride=3), slice(None))] for i in range(3)]

    def take(i, place):
        return jnp.take_along_axis(a[i], place & 127, axis=1, mode="promise_in_bounds")

    second, third, last = 96 + x, 192 + x, 288 + x
    rows = [
        take(0, x),
        jnp.where(second < 128, take(0, second), take(1, second)),
        jnp.where(third < 256, take(1, third), take(2, third)),
        take(2, last),
    ]
    for i, row in enumerate(rows):
        wide_ref[(*to, pl.ds(i, 24, stride=4), slice(None))] = row


def narrow(wide_ref, at):
    lane = lane_of(24)
    o0, o1, o2, o3 = [wide_ref[(*at, pl.ds(i, 24, stride=4), slice(None))] for i in range(4)]
    r1, r2, r3 = roll(o1, 96, 1), roll(o2, 64, 1), roll(o3, 32, 1)
    return (
        jnp.where(lane < 96, o0, r1),
        jnp.where(lane < 64, r1, r2),
        jnp.where(lane < 32, r2, r3),
    )


def put(rows, *targets):
    for ref, to in targets:
        for i in range(3):
            ref[(*to, pl.ds(i, 24, stride=3), slice(None))] = rows[i]


def along(values, axis):
    values = values + roll(values, 1, axis)
    return values + roll(values, -1, axis)


def operator(u, e, turned, d):
    mid = e[1] * u[1]
    once = along((u[0] + u[2]) + (u[1] + u[1]), 0)
    twice = along((e[0] * u[0] + e[2] * u[2]) + (mid + mid), 0)
    both = e[1] * once + twice
    sides = roll(turned[0] * once + twice, -1, 1) + roll(turned[1] * once + twice, 1, 1)
    return d * u[1] - (both + both) - sides


def diagonal(e):
    return 64.4 * e[1] + along(along((e[0] + e[2]) + (e[1] + e[1]), 0), 1)


def prepare(j, e, d, turned):
    d[j] = diagonal(e)
    turned[0, j] = roll(e[1], 1, 1)
    turned[1, j] = roll(e[1], -1, 1)


def three(ref, *at):
    *lead, mid = at
    return [ref[(*lead, mid + k)] for k in (-1, 0, 1)]


def total(values):
    return jnp.sum(jnp.sum(values, axis=0, keepdims=True), axis=1, keepdims=True)


def fold(values):
    out = values[0:8]
    for i in range(8, values.shape[0], 8):
        out = out + values[i : i + 8]
    return out


def pick(row, lane, k):
    return jnp.sum(jnp.where(lane == k, row, 0.0), axis=1, keepdims=True)


def on_plane_loop(count, body):
    lax.fori_loop(0, count, lambda i, c: (body(i), c)[1], 0)


def map_kernel(
    ids,
    counts_in,
    *refs,
):
    _map_kernel(ids, counts_in, refs[:7], *refs[7:])


def _map_kernel(
    ids,
    counts_in,
    sources,
    inner,
    outer,
    own,
    pull,
    e_wide,
    history,
    dev,
    extra,
    flat,
    wide,
    counts,
    plastic,
    hard,
    begin,
    delta,
    shear,
    bulk,
    yields,
    count_sem,
    sems,
):
    def copies(z):
        out = []
        for k, (source, target) in enumerate(zip(sources, targets)):
            at = (slice(None), z) if len(source.shape) == 4 else (z,)
            out.append(pltpu.make_async_copy(source.at[at], target.at[at], sems.at[z, k]))
        return out

    targets = (plastic, hard, begin, delta, shear, bulk, yields)
    get_counts = pltpu.make_async_copy(counts_in, counts, count_sem)
    get_counts.start()
    for z in range(DEPTH):
        for copy in copies(z):
            copy.start()
    get_counts.wait()
    group, first = ids[0], ids[1] * BLOCKS
    row = lax.broadcasted_iota(jnp.int32, (FLAT, LANES), 0)

    def plane(z):
        for copy in copies(z):
            copy.wait()
        block = [counts[group, first + 4 * z + b] for b in range(4)]
        turns = jnp.maximum(jnp.maximum(block[0], block[1]), jnp.maximum(block[2], block[3]))
        held = jnp.where(
            row < 2 * BLOCK_ROWS,
            jnp.where(row < BLOCK_ROWS, block[0], block[1]),
            jnp.where(row < 3 * BLOCK_ROWS, block[2], block[3]),
        )
        share = 1.0 / held.astype(F32)
        twice_mu = 2.0 * shear[z]
        elastic = [begin[i, z] - plastic[i, z] for i in range(6)]
        step = [delta[i, z] for i in range(6)]
        third0 = (elastic[0] + elastic[1] + elastic[2]) * (1.0 / 3.0)
        third1 = (step[0] + step[1] + step[2]) * (1.0 / 3.0)
        stress = [twice_mu * (elastic[i] - third0 if i < 3 else elastic[i]) for i in range(6)]
        rate = twice_mu * share
        for i in range(6):
            flat[i] = rate * (step[i] - third1 if i < 3 else step[i])
        floor = root_two_thirds * yields[z]
        limit0 = floor + (root_two_thirds * 0.15) * twice_mu * hard[z]
        most = 1.0 / floor

        def substep(t, carry):
            *s, gone, _, _ = carry
            act = jnp.where(held >= turns - t, 1.0, 0.0)
            s = [s[i] + act * flat[i] for i in range(6)]
            square = s[0] * s[0]
            for i in range(1, 6):
                square = square + s[i] * s[i]
            square = jnp.maximum(square, 1e-30)
            inverse = lax.rsqrt(square)
            over = jnp.maximum(square * inverse - (limit0 + HARDEN * gone), 0.0) * act
            inverse = jnp.minimum(inverse, most)
            theta = 1.0 - (RETURN * over) * inverse
            return (*[theta * s[i] for i in range(6)], gone + over, theta, inverse)

        zero = jnp.zeros((FLAT, LANES), F32)
        *s, gone, theta, inverse = lax.fori_loop(0, turns, substep, (*stress, zero, zero, zero))
        mu = 0.5 * twice_mu
        per = 1.0 / twice_mu
        elastic = [begin[i, z] - plastic[i, z] + delta[i, z] for i in range(6)]
        trace = elastic[0] + elastic[1] + elastic[2]
        third = trace * (1.0 / 3.0)
        for i in range(6):
            whole = elastic[i] - third if i < 3 else elastic[i]
            history[i, z] = plastic[i, z] + (whole - per * s[i])
            dev[i, z] = s[i]
        history[6, z] = hard[z] + (root_two_thirds / 1.1) * per * gone
        pressure = bulk[z] * trace
        ratio = inverse / theta
        coef = mu * theta
        extra[0, z] = pressure
        extra[1, z] = mu * (theta - 1.0) * (ratio * ratio)
        extra[2, z] = coef
        for i in range(6):
            flat[i] = pressure + s[i] if i < 3 else s[i]
        flat[6] = coef * (1.0 / 128.0)
        for i in range(7):
            widen(flat, (i,), wide, (i,))
        e_wide[z] = wide[6]

        def along_x(u):
            return roll(u, -1, 1) - roll(u, 1, 1)

        def along_y(u):
            return roll(u, -1, 0) - roll(u, 1, 0)

        half = 0.5 * half_root
        own[0, z] = 0.5 * along_x(wide[0]) + half * along_y(wide[5])
        own[1, z] = half * along_x(wide[5]) + 0.5 * along_y(wide[1])
        own[2, z] = half * (along_x(wide[4]) + along_y(wide[3]))
        pull[0, z] = half * wide[4]
        pull[1, z] = half * wide[3]
        pull[2, z] = 0.5 * wide[2]

    for z in range(DEPTH):
        plane(z)

    for c in range(3):
        own[c, 0] = own[c, 0] + pull[c, 1]
        own[c, 1] = own[c, 1] + pull[c, 2] - pull[c, 0]
        own[c, 2] = own[c, 2] - pull[c, 1]
    facing = 2 - 2 * lax.rem(ids[1], 2)
    for ref, near in ((inner, facing), (outer, 2 - facing)):
        for c in range(3):
            ref[c] = own[c, near]
            ref[3 + c] = own[c, 1]
            ref[6 + c] = pull[c, near]
        ref[9] = e_wide[near]
        ref[10] = e_wide[1]
        ref[11] = e_wide[2 - near]


def sums_kernel(ids, pull_group, pull_block, dev, extra, bulk, history, _, *sends):
    group, slab = ids[0], ids[1]
    lane = lane_of(1)
    pairs = [(i, j) for i in range(6) for j in range(i, 6)]

    def chunk(t, carry):
        z, at = t // 3, pl.multiple_of((t % 3) * 24, 8)
        rows = pl.ds(at, 24)
        s = [dev[i, z, rows] for i in range(6)]
        pressure = extra[0, z, rows]
        weighted = extra[1, z, rows]
        terms = [pressure + s[i] if i < 3 else s[i] for i in range(6)]
        terms += [bulk[z, rows], extra[2, z, rows]]
        ws = [weighted * v for v in s]
        terms += [ws[i] * s[j] for i, j in pairs]
        return tuple(c + fold(v) for c, v in zip(carry, terms))

    zero = jnp.zeros((8, LANES), F32)
    sums = lax.fori_loop(0, 9, chunk, (zero,) * (8 + len(pairs)))
    sums = [total(v) * (1.0 / VOXELS) for v in sums]
    row = jnp.zeros((1, LANES), F32)
    for i in range(6):
        row = jnp.where(lane == i, sums[i], row)
    row = jnp.where(lane == BULK_LANE, sums[6], row)
    row = jnp.where(lane == COEF_LANE, sums[7], row)
    for k, (i, j) in enumerate(pairs):
        hit = (lane == 6 + 6 * i + j) | (lane == 6 + 6 * j + i)
        row = jnp.where(hit, sums[8 + k], row)

    for shift in range(4):
        to = lax.rem(group + shift, 4)
        first = pull_group[to, 2 * slab] == group
        at = jnp.where(first, pull_block[to, 2 * slab], pull_block[to, 2 * slab + 1])
        at = jnp.clip(at - slab * BLOCKS, 0, BLOCKS - 1)
        z, part = at // 4, at % 4
        for b in range(4):

            @pl.when(part == b)
            def _():
                for i in range(7):
                    block = history[i, z, pl.ds(BLOCK_ROWS * b, BLOCK_ROWS)]
                    sends[shift][i, 0:BLOCK_ROWS] = block

        sends[shift][7, 0:1] = row


def rows_kernel(ids, owner, kept, from1, from2, from3, summed):
    row = jnp.zeros((1, LANES), F32)
    for shift, source in enumerate((kept, from1, from2, from3)):
        mine = owner[lax.rem(ids[0] - shift + 4, 4)] == ids[0]
        row = row + jnp.where(mine, source[7, 0:1], 0.0)
    summed[...] = row


def inbox_kernel(ids, pull_group, kept, from1, from2, from3, _, inbox):
    group, slab = ids[0], ids[1]
    sources = (kept, from1, from2, from3)
    for slot in range(2):
        away = lax.rem(group - pull_group[group, 2 * slab + slot] + 4, 4)
        for shift in range(4):

            @pl.when(away == shift)
            def _():
                for i in range(7):
                    inbox[i, pl.ds(slot, BLOCK_ROWS, stride=2)] = sources[shift][i, 0:BLOCK_ROWS]


def sides_of(ids):
    above = 1 - lax.rem(ids[1], 2)
    sign = jnp.where(above == 1, 1.0, -1.0)
    return above, 2 * above, 2 - 2 * above, sign


def outer_kernel(ids, inner, own, pull, message):
    _, facing, _, sign = sides_of(ids)
    for c in range(3):
        message[c] = own[c, facing] + sign * inner[6 + c]
        message[3 + c] = inner[c] - sign * pull[c, facing]
        message[6 + c] = inner[3 + c]
    message[9] = inner[9]
    message[10] = inner[10]


def inner_kernel(ids, outer, own, pull, _0, _1, message):
    _, _, edge, sign = sides_of(ids)
    for c in range(3):
        message[c] = own[c, edge] - sign * outer[6 + c]
        message[3 + c] = outer[c] + sign * pull[c, edge]
        message[6 + c] = outer[3 + c]
    message[9] = outer[9]
    message[10] = outer[10]


def first_kernel(ids, inner, outer, own, pull, e_own, p0, p1, p2, e, moments, d, turned):
    above = 1 - lax.rem(ids[1], 2)
    for c in range(3):
        p0[c, 3] = own[c, 1]
    for z in range(3):
        e[2 + z] = e_own[z]
    for ref, high in ((inner, above), (outer, 1 - above)):
        sign = jnp.where(high == 1, 1.0, -1.0)
        for c in range(3):
            p0[c, 6 * high] = ref[3 + c]
            p0[c, 1 + 4 * high] = ref[c] - sign * pull[c, 2 * high]
            p0[c, 2 + 2 * high] = own[c, 2 * high] + sign * ref[6 + c]
        e[6 * high] = ref[10]
        e[1 + 4 * high] = ref[9]

    for j in range(5):
        ee = three(e, j + 1)
        prepare(j, ee, d, turned)
        sides = (turned[0, j], turned[1, j])
        for c in range(3):
            p1[c, j] = operator(three(p0, c, j + 1), ee, sides, d[j])

    sums = [jnp.zeros((8, LANES), F32)] * 4
    for z in range(3):
        ee = three(e, z + 2)
        sides = (turned[0, z + 1], turned[1, z + 1])
        for c in range(3):
            new = operator(three(p1, c, z + 1), ee, sides, d[z + 1])
            p2[z, c] = new
            r0, r1 = p0[c, z + 2], p1[c, z + 1]
            terms = (r0 * r0, r0 * r1, r1 * r1, r1 * new)
            sums = [a + fold(v) for a, v in zip(sums, terms)]
    lane = lane_of(1)
    keep = lane_of(8) < NVX
    row = jnp.zeros((1, LANES), F32)
    for k in range(4):
        row = jnp.where(lane == k, total(jnp.where(keep, sums[k], 0.0)), row)
    moments[...] = row


def lanczos(m0, m1, m2, m3):
    over = jnp.where(m0 > 0.0, m0, 1.0)
    a0 = jnp.clip(m1 / over, 0.0, 2.1)
    left = jnp.maximum(m2 - 2.0 * a0 * m1 + a0 * a0 * m0, 1e-7 * m2)
    b1 = jnp.clip(left / over, 0.0, 1.2)
    left = jnp.where(left > 0.0, left, 1.0)
    a1 = jnp.clip((m3 - 2.0 * a0 * m2 + a0 * a0 * m1) / left, 0.0, 2.1)
    return a0, a1, b1


class Planes:
    def __init__(self, middle, first, count, far=None, width=0):
        self.middle, self.first, self.count, self.far, self.width = middle, first, count, far, width

    def at(self, k):
        i = k - self.first
        if 0 <= i < self.count:
            return self.middle, i
        return self.far, i + self.width if i < 0 else self.width + i - self.count

    def get(self, k, *lead):
        ref, i = self.at(k)
        return ref[(*lead, i)]

    def set(self, k, value, *lead):
        ref, i = self.at(k)
        ref[(*lead, i)] = value

    def three(self, k, *lead):
        return [self.get(k + i, *lead) for i in (-1, 0, 1)]


def second_kernel(
    ids,
    moments,
    summed,
    inner1,
    outer1,
    inner,
    outer,
    p0_in,
    p1_in,
    p2_in,
    e_in,
    d_in,
    turned_in,
    basis,
    gram,
    p0_far,
    p1_far,
    p2_far,
    e_far,
    d_far,
    turned_far,
    v1_all,
    v2_all,
    v3_all,
    v4_all,
):
    p0 = Planes(p0_in, -2, 7, p0_far, 3)
    p1 = Planes(p1_in, -1, 5, p1_far, 3)
    e = Planes(e_in, -2, 7, e_far, 3)
    d = Planes(d_in, -1, 5, d_far, 3)
    turned = Planes(turned_in, -1, 5, turned_far, 3)
    p2 = Planes(None, 0, 3, p2_far, 3)
    v1 = Planes(v1_all, -2, 7)
    v2 = Planes(v2_all, -3, 9)
    v3 = Planes(v3_all, -2, 7)
    v4 = Planes(v4_all, -1, 5)

    lane = lane_of(1)
    found = [pick(moments[...], lane, k) for k in range(4)]
    a0, a1, b1 = lanczos(*found)
    c1, c0 = -(a0 + a1), a0 * a1 - b1
    above = 1 - lax.rem(ids[1], 2)
    for near, ref, high in ((inner1, inner, above), (outer1, outer, 1 - above)):
        for k in range(3):
            place = 2 - k + high * (1 + 2 * k)
            for c in range(3):
                p0_far[c, place] = ref[3 * k + c]
            e_far[place] = near[11] if k == 0 else ref[8 + k]

    far1, far2 = (-4, -3, -2, 4, 5, 6), (-3, -2, -1, 3, 4, 5)
    for k in far1:
        ee = e.three(k)
        d.set(k, diagonal(ee))
        turned.set(k, roll(ee[1], 1, 1), 0)
        turned.set(k, roll(ee[1], -1, 1), 1)

    def apply(field, k, c):
        u = field.three(k, c)
        return u[1], operator(u, e.three(k), (turned.get(k, 0), turned.get(k, 1)), d.get(k))

    for k in far1:
        for c in range(3):
            p1.set(k, apply(p0, k, c)[1], c)
    for k in far2:
        for c in range(3):
            p2.set(k, apply(p1, k, c)[1], c)
    for k in range(-3, 6):
        for c in range(3):
            r0, r1 = p0.get(k, c), p1.get(k, c)
            r2 = p2_in[k, c] if 0 <= k < 3 else p2.get(k, c)
            v2.set(k, r2 + c1 * r1 + c0 * r0, c)
            if -2 <= k <= 4:
                v1.set(k, r1 - a0 * r0, c)
    for k in range(-2, 5):
        for c in range(3):
            mid, new = apply(v2, k, c)
            v3.set(k, new - a1 * mid - b1 * v1.get(k, c), c)
    for k in range(-1, 4):
        for c in range(3):
            mid, new = apply(v3, k, c)
            v4.set(k, new - a1 * mid - b1 * v2.get(k, c), c)

    sums = [jnp.zeros((8, LANES), F32)] * len(PAIRS)
    for z in range(3):
        for c in range(3):
            mid, new = apply(v4, z, c)
            vectors = [p0.get(z, c), v1.get(z, c), v2.get(z, c), v3.get(z, c), mid, new]
            for k in range(5):
                basis[k, c, z] = vectors[k]
            sums = [a + fold(vectors[i] * vectors[j]) for a, (i, j) in zip(sums, PAIRS)]
    keep = lane_of(8) < NVX
    row = pltpu.roll(jnp.broadcast_to(summed[...], (8, LANES)), SUM_BASE, 1)[0:1]
    sent = [total(jnp.where(keep, v, 0.0)) for v in sums] + [a0, a1, b1] + found
    for k, value in enumerate(sent):
        row = jnp.where(lane == k, value, row)
    gram[...] = jnp.broadcast_to(row, (32, LANES))


def plus(x, y):
    return y if x is None else x if y is None else x + y


def times(x, y):
    if x is None or y is None:
        return None
    return y if isinstance(x, float) else x if isinstance(y, float) else x * y


def inner(g, x, y):
    out = None
    for i in range(6):
        part = None
        for j in range(6):
            part = plus(part, times(g.get((min(i, j), max(i, j))), y[j]))
        out = plus(out, times(x[i], part))
    return out


def minus(x, y):
    return x if y is None else -y if x is None else x - y


def basis_change(own, common):
    a0, a1, b1 = own
    c0, c1, d1 = common
    diag = (a0, a1, a1, a1)
    rows = [[1.0] + [None] * 5, [a0 - c0, 1.0] + [None] * 4]
    for k in range(1, 4):
        last, before, row = rows[k], rows[k - 1], [None] * 6
        for j in range(k + 2):
            value = last[j - 1] if j >= 1 else None
            if j <= 3 and last[j] is not None:
                value = plus(value, times(diag[j] - c1, last[j]))
            if j <= 2:
                value = plus(value, times(b1, last[j + 1]))
            row[j] = minus(value, times(d1, before[j]))
        rows.append(row)
    last, row = rows[4], [None] * 6
    for j in range(5):
        row[j + 1] = plus(row[j + 1], last[j])
        if j <= 3:
            row[j] = plus(row[j], times(diag[j], last[j]))
        if 1 <= j <= 3:
            row[j - 1] = plus(row[j - 1], times(b1, last[j]))
    return rows + [row]


def last_kernel(ids, gram, basis, correction, sums, wide):
    table = gram[...]
    row = jnp.sum(table, axis=0, keepdims=True)
    lane = lane_of(1)
    sides = jnp.concatenate([table, jnp.zeros((LANES - 32, LANES), F32)], axis=0).T
    entry = [sides[k : k + 1] for k in range(len(PAIRS) + 7)]
    own = entry[len(PAIRS) : len(PAIRS) + 3]
    a0, a1, b1 = lanczos(*[jnp.sum(v, axis=1, keepdims=True) for v in entry[len(PAIRS) + 3 :]])
    change = basis_change(own, (a0, a1, b1))
    local = {pair: entry[k] for k, pair in enumerate(PAIRS)}

    def dot(x, y):
        out = None
        for u, v in zip(x, y):
            out = plus(out, times(u, v))
        return out

    half = [[dot(change[k], [local.get((min(j, m), max(j, m))) for j in range(6)]) for m in range(6)] for k in range(5)]
    g = {(k, m): jnp.sum(dot(half[k], change[m]), axis=1, keepdims=True) for k, m in PAIRS}
    one = jnp.ones((1, 1), F32)

    def act(v):
        out = [None] * 6
        diag = (a0, a1, a1, a1, None)
        for i in range(5):
            out[i + 1] = plus(out[i + 1], v[i])
            out[i] = plus(out[i], times(diag[i], v[i]))
            if 1 <= i <= 3:
                out[i - 1] = plus(out[i - 1], times(b1, v[i]))
        return out

    found = [None] * 6
    residual = [one] + [None] * 5
    direction = [one] + [None] * 5
    norm = g[0, 0]
    for turn in range(5):
        image = act(direction)
        alpha = norm / inner(g, direction, image)
        found = [plus(x, times(alpha, v)) for x, v in zip(found, direction)]
        if turn < 4:
            residual = [plus(x, times(-alpha, v)) for x, v in zip(residual, image)]
            new = inner(g, residual, residual)
            beta = new / norm
            direction = [plus(x, times(beta, v)) for x, v in zip(residual, direction)]
            norm = new
    weights = []
    for j in range(5):
        value = jnp.broadcast_to(dot(found[:5], [change[k][j] for k in range(5)]), (1, LANES))
        weights.append(pick(value, lane, ids[1]) * (1.0 / 16.0))

    def plane(z):
        for c in range(3):
            out = weights[0] * basis[0, c, z]
            for k in range(1, 5):
                out = out + weights[k] * basis[k, c, z]
            wide[c] = out
            put(narrow(wide, (c,)), (correction, (c, z)))

    on_plane_loop(DEPTH, plane)

    bulk = pick(row, lane, SUM_BASE + BULK_LANE)
    coef = pick(row, lane, SUM_BASE + COEF_LANE)
    shifted = pltpu.roll(jnp.broadcast_to(row, (8, LANES)), LANES - SUM_BASE, 1)[0:1]
    entry = lane - 6
    i, j = entry // 6, entry % 6
    tangent = (lane >= 6) & (lane < 42)
    normal = tangent & (i < 3) & (j < 3)
    out = jnp.where(tangent, 2.0 * shifted, shifted)
    out = out + jnp.where(tangent & (i == j), 2.0 * coef, 0.0)
    out = out + jnp.where(normal, bulk - (2.0 / 3.0) * coef, 0.0)
    sums[...] = out


def shape(*dims):
    return jax.ShapeDtypeStruct(dims, F32)


def near(*dims):
    return pltpu.VMEM(dims, F32)


def far(*dims):
    return pltpu.HBM(dims, F32)


def in_hbm(array):
    return pltpu.with_memory_space_constraint(array, pltpu.HBM)


VM = pl.BlockSpec(memory_space=pltpu.VMEM)
SM = pl.BlockSpec(memory_space=pltpu.SMEM)
HB = pl.BlockSpec(memory_space=pltpu.HBM)
ANY = pl.BlockSpec(memory_space=pl.ANY)


def call(kernel, in_specs, outs, scratch, args, flops, name, limit=12, out_specs=None):
    size = sum(4 * math.prod(a.shape) for a in (*args, *outs))
    return pl.pallas_call(
        kernel,
        out_shape=tuple(outs),
        in_specs=in_specs,
        out_specs=tuple(out_specs or (VM,) * len(outs)),
        scratch_shapes=[pltpu.VMEM(s, F32) if isinstance(s, tuple) else s for s in scratch],
        compiler_params=pltpu.CompilerParams(vmem_limit_bytes=limit * 2**20),
        cost_estimate=pl.CostEstimate(flops=flops, bytes_accessed=size, transcendentals=0),
        name=name,
    )(*args)


def on_device(
    plastic_strain,
    hardening_var,
    strain_start,
    strain_step,
    shear_mod,
    bulk_mod,
    yield_stress,
    substeps,
    pull_group,
    pull_block,
    owner,
):
    slabs = lax.axis_size("slab")
    ids = jnp.stack([lax.axis_index("rve"), lax.axis_index("slab")]).astype(jnp.int32)
    six = [a.reshape(6, DEPTH, FLAT, LANES) for a in (plastic_strain, strain_start, strain_step)]
    one = [a.reshape(DEPTH, FLAT, LANES) for a in (hardening_var, shear_mod, bulk_mod, yield_stress)]
    plane = (FLAT, LANES)
    wide = (NVX, LANES)

    inner, outer, own, pull, e_own, history, dev, extra = call(
        map_kernel,
        [SM] + [HB] * 8,
        [
            shape(FIRST, *wide),
            shape(FIRST, *wide),
            shape(3, 3, *wide),
            shape(3, 3, *wide),
            shape(3, *wide),
            shape(7, 3, *plane),
            shape(6, 3, *plane),
            shape(3, 3, *plane),
        ],
        [
            pltpu.VMEM((7, *plane), F32),
            pltpu.VMEM((7, *wide), F32),
            pltpu.SMEM((4, 384), jnp.int32),
            pltpu.VMEM((6, DEPTH, *plane), F32),
            pltpu.VMEM((DEPTH, *plane), F32),
            pltpu.VMEM((6, DEPTH, *plane), F32),
            pltpu.VMEM((6, DEPTH, *plane), F32),
            pltpu.VMEM((DEPTH, *plane), F32),
            pltpu.VMEM((DEPTH, *plane), F32),
            pltpu.VMEM((DEPTH, *plane), F32),
            pltpu.SemaphoreType.DMA,
            pltpu.SemaphoreType.DMA((DEPTH, 7)),
        ],
        (ids, *map(in_hbm, (substeps, six[0], one[0], six[1], six[2], one[1], one[2], one[3]))),
        5_000_000,
        "return_map",
    )
    on_chip = [(i, i ^ 1) for i in range(slabs)]
    across = [(i, (i + 1 if i % 2 else i - 1) % slabs) for i in range(slabs)]
    outer1 = lax.ppermute(outer, "slab", across)
    inner1 = lax.ppermute(inner, "slab", on_chip)
    (outer,) = call(
        outer_kernel,
        [SM] + [VM] * 3,
        [shape(SECOND, *wide)],
        [],
        (ids, inner1, own, pull),
        500_000,
        "to_outer",
    )
    outer2 = lax.ppermute(outer, "slab", across)
    kept, *sends = call(
        sums_kernel,
        [SM, SM, SM] + [VM] * 4 + [ANY],
        [shape(8, 24, LANES)] * 4,
        [],
        (ids, pull_group, pull_block, dev, extra, one[2], history, outer),
        2_000_000,
        "element_partials",
    )
    came = [
        lax.ppermute(sends[k - 1], "rve", [(i, (i + k) % 4) for i in range(4)]) for k in (1, 2, 3)
    ]

    (inner,) = call(
        inner_kernel,
        [SM] + [VM] * 3 + [ANY] * 2,
        [shape(SECOND, *wide)],
        [],
        (ids, outer1, own, pull, kept, came[1]),
        500_000,
        "to_inner",
    )
    inner2 = lax.ppermute(inner, "slab", on_chip)

    p0, p1, p2, e, moments, d, turned = call(
        first_kernel,
        [SM] + [VM] * 5,
        [
            shape(3, 7, *wide),
            shape(3, 5, *wide),
            shape(3, 3, *wide),
            shape(7, *wide),
            shape(1, LANES),
            shape(5, *wide),
            shape(2, 5, *wide),
        ],
        [],
        (ids, inner1, outer1, own, pull, e_own),
        5_000_000,
        "basis_first",
    )
    (summed,) = call(
        rows_kernel,
        [SM, SM] + [VM] * 4,
        [shape(1, LANES)],
        [],
        (ids, owner, kept, *came),
        100_000,
        "rows",
    )
    basis, gram = call(
        second_kernel,
        [SM] + [VM] * 12,
        [shape(5, 3, 3, *wide), shape(32, LANES)],
        [
            (3, 6, *wide),
            (3, 6, *wide),
            (3, 6, *wide),
            (6, *wide),
            (6, *wide),
            (2, 6, *wide),
            (3, 7, *wide),
            (3, 9, *wide),
            (3, 7, *wide),
            (3, 5, *wide),
        ],
        (ids, moments, summed, inner1, outer1, inner2, outer2, p0, p1, p2, e, d, turned),
        12_000_000,
        "basis_second",
    )
    (inbox,) = call(
        inbox_kernel,
        [SM, SM] + [VM] * 4 + [ANY],
        [shape(7, 2 * BLOCK_ROWS, LANES)],
        [],
        (ids, pull_group, kept, *came, basis),
        100_000,
        "inbox",
    )
    gram = lax.all_to_all(gram, "slab", split_axis=0, concat_axis=0, tiled=True)
    correction, element = call(
        last_kernel,
        [SM, VM, VM],
        [shape(3, 3, *plane), shape(1, LANES)],
        [(3, *wide)],
        (ids, gram, basis),
        1_000_000,
        "combine",
    )
    inbox = inbox.reshape(7, BLOCK_ROWS, 2, LANES).transpose(0, 2, 1, 3)
    return (
        correction.reshape(3, 1, DEPTH, FLAT * LANES),
        inbox.reshape(7, 1, 2, BLOCK_ROWS * LANES),
        element[:, :42],
    )


def solution(mesh):
    return jax.shard_map(
        on_device,
        mesh=mesh,
        in_specs=(
            P(None, "rve", "slab", None),
            P("rve", "slab", None),
            P(None, "rve", "slab", None),
            P(None, "rve", "slab", None),
            P("rve", "slab", None),
            P("rve", "slab", None),
            P("rve", "slab", None),
            P(),
            P(),
            P(),
            P(),
        ),
        out_specs=(P(None, "rve", "slab", None), P(None, "rve", "slab", None), P("rve", None)),
        check_vma=False,
    )
```

```python
import math

import jax
import jax.numpy as jnp
from jax import lax
from jax.experimental import pallas as pl
from jax.experimental.pallas import tpu as pltpu
from jax.sharding import PartitionSpec as P

NVX = 96
LANES = 128
FLAT = 72
DEPTH = 3
BLOCK_ROWS = 18
BLOCKS = 12
VOXELS = 884736.0
F32 = jnp.float32

root_two_thirds = math.sqrt(2.0 / 3.0)
half_root = 1.0 / math.sqrt(2.0)
RETURN = 2.0 / 2.2
HARDEN = 0.2 / 2.2

BULK_LANE = 42
COEF_LANE = 43
SUM_BASE = 64
PAIRS = [(i, j) for i in range(6) for j in range(i, 6) if (i, j) != (5, 5)]

FIRST = 12
SECOND = 11


def roll(values, shift, axis):
    return pltpu.roll(values, shift % values.shape[axis], axis)


def lane_of(rows):
    return lax.broadcasted_iota(jnp.int32, (rows, LANES), 1)


def widen(flat_ref, at, wide_ref, to):
    lane = lane_of(24)
    x = jnp.where(lane < 96, lane, jnp.where(lane < 112, lane - 96, lane - 32))
    a = [flat_ref[(*at, pl.ds(i, 24, stride=3), slice(None))] for i in range(3)]

    def take(i, place):
        return jnp.take_along_axis(a[i], place & 127, axis=1, mode="promise_in_bounds")

    second, third, last = 96 + x, 192 + x, 288 + x
    rows = [
        take(0, x),
        jnp.where(second < 128, take(0, second), take(1, second)),
        jnp.where(third < 256, take(1, third), take(2, third)),
        take(2, last),
    ]
    for i, row in enumerate(rows):
        wide_ref[(*to, pl.ds(i, 24, stride=4), slice(None))] = row


def narrow(wide_ref, at):
    lane = lane_of(24)
    o0, o1, o2, o3 = [wide_ref[(*at, pl.ds(i, 24, stride=4), slice(None))] for i in range(4)]
    r1, r2, r3 = roll(o1, 96, 1), roll(o2, 64, 1), roll(o3, 32, 1)
    return (
        jnp.where(lane < 96, o0, r1),
        jnp.where(lane < 64, r1, r2),
        jnp.where(lane < 32, r2, r3),
    )


def put(rows, *targets):
    for ref, to in targets:
        for i in range(3):
            ref[(*to, pl.ds(i, 24, stride=3), slice(None))] = rows[i]


def along(values, axis):
    values = values + roll(values, 1, axis)
    return values + roll(values, -1, axis)


def operator(u, e, turned, d):
    mid = e[1] * u[1]
    once = along((u[0] + u[2]) + (u[1] + u[1]), 0)
    twice = along((e[0] * u[0] + e[2] * u[2]) + (mid + mid), 0)
    both = e[1] * once + twice
    sides = roll(turned[0] * once + twice, -1, 1) + roll(turned[1] * once + twice, 1, 1)
    return d * u[1] - (both + both) - sides


def diagonal(e):
    return 64.4 * e[1] + along(along((e[0] + e[2]) + (e[1] + e[1]), 0), 1)


def prepare(j, e, d, turned):
    d[j] = diagonal(e)
    turned[0, j] = roll(e[1], 1, 1)
    turned[1, j] = roll(e[1], -1, 1)


def three(ref, *at):
    *lead, mid = at
    return [ref[(*lead, mid + k)] for k in (-1, 0, 1)]


def total(values):
    return jnp.sum(jnp.sum(values, axis=0, keepdims=True), axis=1, keepdims=True)


def fold(values):
    out = values[0:8]
    for i in range(8, values.shape[0], 8):
        out = out + values[i : i + 8]
    return out


def pick(row, lane, k):
    return jnp.sum(jnp.where(lane == k, row, 0.0), axis=1, keepdims=True)


def on_plane_loop(count, body):
    lax.fori_loop(0, count, lambda i, c: (body(i), c)[1], 0)


def map_kernel(
    ids,
    counts_in,
    *refs,
):
    _map_kernel(ids, counts_in, refs[:7], *refs[7:])


def _map_kernel(
    ids,
    counts_in,
    sources,
    inner,
    outer,
    own,
    pull,
    e_wide,
    history,
    dev,
    extra,
    flat,
    wide,
    counts,
    plastic,
    hard,
    begin,
    delta,
    shear,
    bulk,
    yields,
    count_sem,
    sems,
):
    def copies(z):
        out = []
        for k, (source, target) in enumerate(zip(sources, targets)):
            at = (slice(None), z) if len(source.shape) == 4 else (z,)
            out.append(pltpu.make_async_copy(source.at[at], target.at[at], sems.at[z, k]))
        return out

    targets = (plastic, hard, begin, delta, shear, bulk, yields)
    get_counts = pltpu.make_async_copy(counts_in, counts, count_sem)
    get_counts.start()
    for z in range(DEPTH):
        for copy in copies(z):
            copy.start()
    get_counts.wait()
    group, first = ids[0], ids[1] * BLOCKS
    row = lax.broadcasted_iota(jnp.int32, (FLAT, LANES), 0)

    def plane(z):
        for copy in copies(z):
            copy.wait()
        block = [counts[group, first + 4 * z + b] for b in range(4)]
        turns = jnp.maximum(jnp.maximum(block[0], block[1]), jnp.maximum(block[2], block[3]))
        held = jnp.where(
            row < 2 * BLOCK_ROWS,
            jnp.where(row < BLOCK_ROWS, block[0], block[1]),
            jnp.where(row < 3 * BLOCK_ROWS, block[2], block[3]),
        )
        share = 1.0 / held.astype(F32)
        twice_mu = 2.0 * shear[z]
        elastic = [begin[i, z] - plastic[i, z] for i in range(6)]
        step = [delta[i, z] for i in range(6)]
        third0 = (elastic[0] + elastic[1] + elastic[2]) * (1.0 / 3.0)
        third1 = (step[0] + step[1] + step[2]) * (1.0 / 3.0)
        stress = [twice_mu * (elastic[i] - third0 if i < 3 else elastic[i]) for i in range(6)]
        rate = twice_mu * share
        for i in range(6):
            flat[i] = rate * (step[i] - third1 if i < 3 else step[i])
        floor = root_two_thirds * yields[z]
        limit0 = floor + (root_two_thirds * 0.15) * twice_mu * hard[z]
        most = 1.0 / floor

        def substep(t, carry):
            *s, gone, _, _ = carry
            act = jnp.where(held >= turns - t, 1.0, 0.0)
            s = [s[i] + act * flat[i] for i in range(6)]
            square = s[0] * s[0]
            for i in range(1, 6):
                square = square + s[i] * s[i]
            square = jnp.maximum(square, 1e-30)
            inverse = lax.rsqrt(square)
            over = jnp.maximum(square * inverse - (limit0 + HARDEN * gone), 0.0) * act
            inverse = jnp.minimum(inverse, most)
            theta = 1.0 - (RETURN * over) * inverse
            return (*[theta * s[i] for i in range(6)], gone + over, theta, inverse)

        zero = jnp.zeros((FLAT, LANES), F32)
        *s, gone, theta, inverse = lax.fori_loop(0, turns, substep, (*stress, zero, zero, zero))
        mu = 0.5 * twice_mu
        per = 1.0 / twice_mu
        elastic = [begin[i, z] - plastic[i, z] + delta[i, z] for i in range(6)]
        trace = elastic[0] + elastic[1] + elastic[2]
        third = trace * (1.0 / 3.0)
        for i in range(6):
            whole = elastic[i] - third if i < 3 else elastic[i]
            history[i, z] = plastic[i, z] + (whole - per * s[i])
            dev[i, z] = s[i]
        history[6, z] = hard[z] + (root_two_thirds / 1.1) * per * gone
        pressure = bulk[z] * trace
        ratio = inverse / theta
        coef = mu * theta
        extra[0, z] = pressure
        extra[1, z] = mu * (theta - 1.0) * (ratio * ratio)
        extra[2, z] = coef
        for i in range(6):
            flat[i] = pressure + s[i] if i < 3 else s[i]
        flat[6] = coef * (1.0 / 128.0)
        for i in range(7):
            widen(flat, (i,), wide, (i,))
        e_wide[z] = wide[6]

        def along_x(u):
            return roll(u, -1, 1) - roll(u, 1, 1)

        def along_y(u):
            return roll(u, -1, 0) - roll(u, 1, 0)

        half = 0.5 * half_root
        own[0, z] = 0.5 * along_x(wide[0]) + half * along_y(wide[5])
        own[1, z] = half * along_x(wide[5]) + 0.5 * along_y(wide[1])
        own[2, z] = half * (along_x(wide[4]) + along_y(wide[3]))
        pull[0, z] = half * wide[4]
        pull[1, z] = half * wide[3]
        pull[2, z] = 0.5 * wide[2]

    for z in range(DEPTH):
        plane(z)

    for c in range(3):
        own[c, 0] = own[c, 0] + pull[c, 1]
        own[c, 1] = own[c, 1] + pull[c, 2] - pull[c, 0]
        own[c, 2] = own[c, 2] - pull[c, 1]
    facing = 2 - 2 * lax.rem(ids[1], 2)
    for ref, near in ((inner, facing), (outer, 2 - facing)):
        for c in range(3):
            ref[c] = own[c, near]
            ref[3 + c] = own[c, 1]
            ref[6 + c] = pull[c, near]
        ref[9] = e_wide[near]
        ref[10] = e_wide[1]
        ref[11] = e_wide[2 - near]


def sums_kernel(ids, pull_group, pull_block, dev, extra, bulk, history, _, *sends):
    group, slab = ids[0], ids[1]
    lane = lane_of(1)
    pairs = [(i, j) for i in range(6) for j in range(i, 6)]

    def chunk(t, carry):
        z, at = t // 3, pl.multiple_of((t % 3) * 24, 8)
        rows = pl.ds(at, 24)
        s = [dev[i, z, rows] for i in range(6)]
        pressure = extra[0, z, rows]
        weighted = extra[1, z, rows]
        terms = [pressure + s[i] if i < 3 else s[i] for i in range(6)]
        terms += [bulk[z, rows], extra[2, z, rows]]
        ws = [weighted * v for v in s]
        terms += [ws[i] * s[j] for i, j in pairs]
        return tuple(c + fold(v) for c, v in zip(carry, terms))

    zero = jnp.zeros((8, LANES), F32)
    sums = lax.fori_loop(0, 9, chunk, (zero,) * (8 + len(pairs)))
    sums = [total(v) * (1.0 / VOXELS) for v in sums]
    row = jnp.zeros((1, LANES), F32)
    for i in range(6):
        row = jnp.where(lane == i, sums[i], row)
    row = jnp.where(lane == BULK_LANE, sums[6], row)
    row = jnp.where(lane == COEF_LANE, sums[7], row)
    for k, (i, j) in enumerate(pairs):
        hit = (lane == 6 + 6 * i + j) | (lane == 6 + 6 * j + i)
        row = jnp.where(hit, sums[8 + k], row)

    for shift in range(4):
        to = lax.rem(group + shift, 4)
        first = pull_group[to, 2 * slab] == group
        at = jnp.where(first, pull_block[to, 2 * slab], pull_block[to, 2 * slab + 1])
        at = jnp.clip(at - slab * BLOCKS, 0, BLOCKS - 1)
        z, part = at // 4, at % 4
        for b in range(4):

            @pl.when(part == b)
            def _():
                for i in range(7):
                    block = history[i, z, pl.ds(BLOCK_ROWS * b, BLOCK_ROWS)]
                    sends[shift][i, 0:BLOCK_ROWS] = block

        sends[shift][7, 0:1] = row


def rows_kernel(ids, owner, kept, from1, from2, from3, summed):
    row = jnp.zeros((1, LANES), F32)
    for shift, source in enumerate((kept, from1, from2, from3)):
        mine = owner[lax.rem(ids[0] - shift + 4, 4)] == ids[0]
        row = row + jnp.where(mine, source[7, 0:1], 0.0)
    summed[...] = row


def inbox_kernel(ids, pull_group, kept, from1, from2, from3, _, inbox):
    group, slab = ids[0], ids[1]
    sources = (kept, from1, from2, from3)
    for slot in range(2):
        away = lax.rem(group - pull_group[group, 2 * slab + slot] + 4, 4)
        for shift in range(4):

            @pl.when(away == shift)
            def _():
                for i in range(7):
                    inbox[i, pl.ds(slot, BLOCK_ROWS, stride=2)] = sources[shift][i, 0:BLOCK_ROWS]


def sides_of(ids):
    above = 1 - lax.rem(ids[1], 2)
    sign = jnp.where(above == 1, 1.0, -1.0)
    return above, 2 * above, 2 - 2 * above, sign


def outer_kernel(ids, inner, own, pull, message):
    _, facing, _, sign = sides_of(ids)
    for c in range(3):
        message[c] = own[c, facing] + sign * inner[6 + c]
        message[3 + c] = inner[c] - sign * pull[c, facing]
        message[6 + c] = inner[3 + c]
    message[9] = inner[9]
    message[10] = inner[10]


def inner_kernel(ids, outer, own, pull, _0, _1, message):
    _, _, edge, sign = sides_of(ids)
    for c in range(3):
        message[c] = own[c, edge] - sign * outer[6 + c]
        message[3 + c] = outer[c] + sign * pull[c, edge]
        message[6 + c] = outer[3 + c]
    message[9] = outer[9]
    message[10] = outer[10]


def first_kernel(ids, inner, outer, own, pull, e_own, p0, p1, p2, e, moments, d, turned):
    above = 1 - lax.rem(ids[1], 2)
    for c in range(3):
        p0[c, 3] = own[c, 1]
    for z in range(3):
        e[2 + z] = e_own[z]
    for ref, high in ((inner, above), (outer, 1 - above)):
        sign = jnp.where(high == 1, 1.0, -1.0)
        for c in range(3):
            p0[c, 6 * high] = ref[3 + c]
            p0[c, 1 + 4 * high] = ref[c] - sign * pull[c, 2 * high]
            p0[c, 2 + 2 * high] = own[c, 2 * high] + sign * ref[6 + c]
        e[6 * high] = ref[10]
        e[1 + 4 * high] = ref[9]

    for j in range(5):
        ee = three(e, j + 1)
        prepare(j, ee, d, turned)
        sides = (turned[0, j], turned[1, j])
        for c in range(3):
            p1[c, j] = operator(three(p0, c, j + 1), ee, sides, d[j])

    sums = [jnp.zeros((8, LANES), F32)] * 4
    for z in range(3):
        ee = three(e, z + 2)
        sides = (turned[0, z + 1], turned[1, z + 1])
        for c in range(3):
            new = operator(three(p1, c, z + 1), ee, sides, d[z + 1])
            p2[z, c] = new
            r0, r1 = p0[c, z + 2], p1[c, z + 1]
            terms = (r0 * r0, r0 * r1, r1 * r1, r1 * new)
            sums = [a + fold(v) for a, v in zip(sums, terms)]
    lane = lane_of(1)
    keep = lane_of(8) < NVX
    row = jnp.zeros((1, LANES), F32)
    for k in range(4):
        row = jnp.where(lane == k, total(jnp.where(keep, sums[k], 0.0)), row)
    moments[...] = row


def lanczos(m0, m1, m2, m3):
    over = jnp.where(m0 > 0.0, m0, 1.0)
    a0 = jnp.clip(m1 / over, 0.0, 2.1)
    left = jnp.maximum(m2 - 2.0 * a0 * m1 + a0 * a0 * m0, 1e-7 * m2)
    b1 = jnp.clip(left / over, 0.0, 1.2)
    left = jnp.where(left > 0.0, left, 1.0)
    a1 = jnp.clip((m3 - 2.0 * a0 * m2 + a0 * a0 * m1) / left, 0.0, 2.1)
    return a0, a1, b1


class Planes:
    def __init__(self, middle, first, count, far=None, width=0):
        self.middle, self.first, self.count, self.far, self.width = middle, first, count, far, width

    def at(self, k):
        i = k - self.first
        if 0 <= i < self.count:
            return self.middle, i
        return self.far, i + self.width if i < 0 else self.width + i - self.count

    def get(self, k, *lead):
        ref, i = self.at(k)
        return ref[(*lead, i)]

    def set(self, k, value, *lead):
        ref, i = self.at(k)
        ref[(*lead, i)] = value

    def three(self, k, *lead):
        return [self.get(k + i, *lead) for i in (-1, 0, 1)]


def second_kernel(
    ids,
    moments,
    summed,
    inner1,
    outer1,
    inner,
    outer,
    p0_in,
    p1_in,
    p2_in,
    e_in,
    d_in,
    turned_in,
    basis,
    gram,
    p0_far,
    p1_far,
    p2_far,
    e_far,
    d_far,
    turned_far,
    v1_all,
    v2_all,
    v3_all,
    v4_all,
):
    p0 = Planes(p0_in, -2, 7, p0_far, 3)
    p1 = Planes(p1_in, -1, 5, p1_far, 3)
    e = Planes(e_in, -2, 7, e_far, 3)
    d = Planes(d_in, -1, 5, d_far, 3)
    turned = Planes(turned_in, -1, 5, turned_far, 3)
    p2 = Planes(None, 0, 3, p2_far, 3)
    v1 = Planes(v1_all, -2, 7)
    v2 = Planes(v2_all, -3, 9)
    v3 = Planes(v3_all, -2, 7)
    v4 = Planes(v4_all, -1, 5)

    lane = lane_of(1)
    found = [pick(moments[...], lane, k) for k in range(4)]
    a0, a1, b1 = lanczos(*found)
    c1, c0 = -(a0 + a1), a0 * a1 - b1
    above = 1 - lax.rem(ids[1], 2)
    for near, ref, high in ((inner1, inner, above), (outer1, outer, 1 - above)):
        for k in range(3):
            place = 2 - k + high * (1 + 2 * k)
            for c in range(3):
                p0_far[c, place] = ref[3 * k + c]
            e_far[place] = near[11] if k == 0 else ref[8 + k]

    far1, far2 = (-4, -3, -2, 4, 5, 6), (-3, -2, -1, 3, 4, 5)
    for k in far1:
        ee = e.three(k)
        d.set(k, diagonal(ee))
        turned.set(k, roll(ee[1], 1, 1), 0)
        turned.set(k, roll(ee[1], -1, 1), 1)

    def apply(field, k, c):
        u = field.three(k, c)
        return u[1], operator(u, e.three(k), (turned.get(k, 0), turned.get(k, 1)), d.get(k))

    for k in far1:
        for c in range(3):
            p1.set(k, apply(p0, k, c)[1], c)
    for k in far2:
        for c in range(3):
            p2.set(k, apply(p1, k, c)[1], c)
    for k in range(-3, 6):
        for c in range(3):
            r0, r1 = p0.get(k, c), p1.get(k, c)
            r2 = p2_in[k, c] if 0 <= k < 3 else p2.get(k, c)
            v2.set(k, r2 + c1 * r1 + c0 * r0, c)
            if -2 <= k <= 4:
                v1.set(k, r1 - a0 * r0, c)
    for k in range(-2, 5):
        for c in range(3):
            mid, new = apply(v2, k, c)
            v3.set(k, new - a1 * mid - b1 * v1.get(k, c), c)
    for k in range(-1, 4):
        for c in range(3):
            mid, new = apply(v3, k, c)
            v4.set(k, new - a1 * mid - b1 * v2.get(k, c), c)

    sums = [jnp.zeros((8, LANES), F32)] * len(PAIRS)
    for z in range(3):
        for c in range(3):
            mid, new = apply(v4, z, c)
            vectors = [p0.get(z, c), v1.get(z, c), v2.get(z, c), v3.get(z, c), mid, new]
            for k in range(5):
                basis[k, c, z] = vectors[k]
            sums = [a + fold(vectors[i] * vectors[j]) for a, (i, j) in zip(sums, PAIRS)]
    keep = lane_of(8) < NVX
    row = pltpu.roll(jnp.broadcast_to(summed[...], (8, LANES)), SUM_BASE, 1)[0:1]
    sent = [total(jnp.where(keep, v, 0.0)) for v in sums] + [a0, a1, b1] + found
    for k, value in enumerate(sent):
        row = jnp.where(lane == k, value, row)
    gram[...] = jnp.broadcast_to(row, (32, LANES))


def plus(x, y):
    return y if x is None else x if y is None else x + y


def times(x, y):
    if x is None or y is None:
        return None
    return y if isinstance(x, float) else x if isinstance(y, float) else x * y


def tree(values):
    values = [v for v in values if v is not None]
    while len(values) > 1:
        values = [plus(*values[i : i + 2]) if i + 1 < len(values) else values[i] for i in range(0, len(values), 2)]
    return values[0] if values else None


def inner(g, x, y):
    parts = [tree([times(g.get((min(i, j), max(i, j))), y[j]) for j in range(6)]) for i in range(6)]
    return tree([times(u, v) for u, v in zip(x, parts)])


def minus(x, y):
    return x if y is None else -y if x is None else x - y


def basis_change(own, common):
    a0, a1, b1 = own
    c0, c1, d1 = common
    diag = (a0, a1, a1, a1)
    rows = [[1.0] + [None] * 5, [a0 - c0, 1.0] + [None] * 4]
    for k in range(1, 4):
        last, before, row = rows[k], rows[k - 1], [None] * 6
        for j in range(k + 2):
            value = last[j - 1] if j >= 1 else None
            if j <= 3 and last[j] is not None:
                value = plus(value, times(diag[j] - c1, last[j]))
            if j <= 2:
                value = plus(value, times(b1, last[j + 1]))
            row[j] = minus(value, times(d1, before[j]))
        rows.append(row)
    last, row = rows[4], [None] * 6
    for j in range(5):
        row[j + 1] = plus(row[j + 1], last[j])
        if j <= 3:
            row[j] = plus(row[j], times(diag[j], last[j]))
        if 1 <= j <= 3:
            row[j - 1] = plus(row[j - 1], times(b1, last[j]))
    return rows + [row]


def last_kernel(ids, gram, basis, correction, sums, wide):
    table = gram[...]
    row = jnp.sum(table, axis=0, keepdims=True)
    lane = lane_of(1)
    sides = jnp.concatenate([table, jnp.zeros((LANES - 32, LANES), F32)], axis=0).T
    entry = [sides[k : k + 1] for k in range(len(PAIRS) + 7)]
    own = entry[len(PAIRS) : len(PAIRS) + 3]
    a0, a1, b1 = lanczos(*[jnp.sum(v, axis=1, keepdims=True) for v in entry[len(PAIRS) + 3 :]])
    change = basis_change(own, (a0, a1, b1))
    local = {pair: entry[k] for k, pair in enumerate(PAIRS)}

    def dot(x, y):
        return tree([times(u, v) for u, v in zip(x, y)])

    half = [[dot(change[k], [local.get((min(j, m), max(j, m))) for j in range(6)]) for m in range(6)] for k in range(5)]
    g = {(k, m): jnp.sum(dot(half[k], change[m]), axis=1, keepdims=True) for k, m in PAIRS}
    one = jnp.ones((1, 1), F32)

    def act(v):
        out = [None] * 6
        diag = (a0, a1, a1, a1, None)
        for i in range(5):
            out[i + 1] = plus(out[i + 1], v[i])
            out[i] = plus(out[i], times(diag[i], v[i]))
            if 1 <= i <= 3:
                out[i - 1] = plus(out[i - 1], times(b1, v[i]))
        return out

    found = [None] * 6
    residual = [one] + [None] * 5
    direction = [one] + [None] * 5
    norm = g[0, 0]
    for turn in range(5):
        image = act(direction)
        alpha = norm / inner(g, direction, image)
        found = [plus(x, times(alpha, v)) for x, v in zip(found, direction)]
        if turn < 4:
            residual = [plus(x, times(-alpha, v)) for x, v in zip(residual, image)]
            new = inner(g, residual, residual)
            beta = new / norm
            direction = [plus(x, times(beta, v)) for x, v in zip(residual, direction)]
            norm = new
    weights = []
    for j in range(5):
        value = jnp.broadcast_to(dot(found[:5], [change[k][j] for k in range(5)]), (1, LANES))
        weights.append(pick(value, lane, ids[1]) * (1.0 / 16.0))

    def plane(z):
        for c in range(3):
            out = weights[0] * basis[0, c, z]
            for k in range(1, 5):
                out = out + weights[k] * basis[k, c, z]
            wide[c] = out
            put(narrow(wide, (c,)), (correction, (c, z)))

    on_plane_loop(DEPTH, plane)

    bulk = pick(row, lane, SUM_BASE + BULK_LANE)
    coef = pick(row, lane, SUM_BASE + COEF_LANE)
    shifted = pltpu.roll(jnp.broadcast_to(row, (8, LANES)), LANES - SUM_BASE, 1)[0:1]
    entry = lane - 6
    i, j = entry // 6, entry % 6
    tangent = (lane >= 6) & (lane < 42)
    normal = tangent & (i < 3) & (j < 3)
    out = jnp.where(tangent, 2.0 * shifted, shifted)
    out = out + jnp.where(tangent & (i == j), 2.0 * coef, 0.0)
    out = out + jnp.where(normal, bulk - (2.0 / 3.0) * coef, 0.0)
    sums[...] = out


def shape(*dims):
    return jax.ShapeDtypeStruct(dims, F32)


def near(*dims):
    return pltpu.VMEM(dims, F32)


def far(*dims):
    return pltpu.HBM(dims, F32)


def in_hbm(array):
    return pltpu.with_memory_space_constraint(array, pltpu.HBM)


VM = pl.BlockSpec(memory_space=pltpu.VMEM)
SM = pl.BlockSpec(memory_space=pltpu.SMEM)
HB = pl.BlockSpec(memory_space=pltpu.HBM)
ANY = pl.BlockSpec(memory_space=pl.ANY)


def call(kernel, in_specs, outs, scratch, args, flops, name, limit=12, out_specs=None):
    size = sum(4 * math.prod(a.shape) for a in (*args, *outs))
    return pl.pallas_call(
        kernel,
        out_shape=tuple(outs),
        in_specs=in_specs,
        out_specs=tuple(out_specs or (VM,) * len(outs)),
        scratch_shapes=[pltpu.VMEM(s, F32) if isinstance(s, tuple) else s for s in scratch],
        compiler_params=pltpu.CompilerParams(vmem_limit_bytes=limit * 2**20),
        cost_estimate=pl.CostEstimate(flops=flops, bytes_accessed=size, transcendentals=0),
        name=name,
    )(*args)


def on_device(
    plastic_strain,
    hardening_var,
    strain_start,
    strain_step,
    shear_mod,
    bulk_mod,
    yield_stress,
    substeps,
    pull_group,
    pull_block,
    owner,
):
    slabs = lax.axis_size("slab")
    ids = jnp.stack([lax.axis_index("rve"), lax.axis_index("slab")]).astype(jnp.int32)
    six = [a.reshape(6, DEPTH, FLAT, LANES) for a in (plastic_strain, strain_start, strain_step)]
    one = [a.reshape(DEPTH, FLAT, LANES) for a in (hardening_var, shear_mod, bulk_mod, yield_stress)]
    plane = (FLAT, LANES)
    wide = (NVX, LANES)

    inner, outer, own, pull, e_own, history, dev, extra = call(
        map_kernel,
        [SM] + [HB] * 8,
        [
            shape(FIRST, *wide),
            shape(FIRST, *wide),
            shape(3, 3, *wide),
            shape(3, 3, *wide),
            shape(3, *wide),
            shape(7, 3, *plane),
            shape(6, 3, *plane),
            shape(3, 3, *plane),
        ],
        [
            pltpu.VMEM((7, *plane), F32),
            pltpu.VMEM((7, *wide), F32),
            pltpu.SMEM((4, 384), jnp.int32),
            pltpu.VMEM((6, DEPTH, *plane), F32),
            pltpu.VMEM((DEPTH, *plane), F32),
            pltpu.VMEM((6, DEPTH, *plane), F32),
            pltpu.VMEM((6, DEPTH, *plane), F32),
            pltpu.VMEM((DEPTH, *plane), F32),
            pltpu.VMEM((DEPTH, *plane), F32),
            pltpu.VMEM((DEPTH, *plane), F32),
            pltpu.SemaphoreType.DMA,
            pltpu.SemaphoreType.DMA((DEPTH, 7)),
        ],
        (ids, *map(in_hbm, (substeps, six[0], one[0], six[1], six[2], one[1], one[2], one[3]))),
        5_000_000,
        "return_map",
    )
    on_chip = [(i, i ^ 1) for i in range(slabs)]
    across = [(i, (i + 1 if i % 2 else i - 1) % slabs) for i in range(slabs)]
    outer1 = lax.ppermute(outer, "slab", across)
    inner1 = lax.ppermute(inner, "slab", on_chip)
    (outer,) = call(
        outer_kernel,
        [SM] + [VM] * 3,
        [shape(SECOND, *wide)],
        [],
        (ids, inner1, own, pull),
        500_000,
        "to_outer",
    )
    outer2 = lax.ppermute(outer, "slab", across)
    kept, *sends = call(
        sums_kernel,
        [SM, SM, SM] + [VM] * 4 + [ANY],
        [shape(8, 24, LANES)] * 4,
        [],
        (ids, pull_group, pull_block, dev, extra, one[2], history, outer),
        2_000_000,
        "element_partials",
    )
    came = [
        lax.ppermute(sends[k - 1], "rve", [(i, (i + k) % 4) for i in range(4)]) for k in (1, 2, 3)
    ]

    (inner,) = call(
        inner_kernel,
        [SM] + [VM] * 3 + [ANY] * 2,
        [shape(SECOND, *wide)],
        [],
        (ids, outer1, own, pull, kept, came[1]),
        500_000,
        "to_inner",
    )
    inner2 = lax.ppermute(inner, "slab", on_chip)

    p0, p1, p2, e, moments, d, turned = call(
        first_kernel,
        [SM] + [VM] * 5,
        [
            shape(3, 7, *wide),
            shape(3, 5, *wide),
            shape(3, 3, *wide),
            shape(7, *wide),
            shape(1, LANES),
            shape(5, *wide),
            shape(2, 5, *wide),
        ],
        [],
        (ids, inner1, outer1, own, pull, e_own),
        5_000_000,
        "basis_first",
    )
    (summed,) = call(
        rows_kernel,
        [SM, SM] + [VM] * 4,
        [shape(1, LANES)],
        [],
        (ids, owner, kept, *came),
        100_000,
        "rows",
    )
    basis, gram = call(
        second_kernel,
        [SM] + [VM] * 12,
        [shape(5, 3, 3, *wide), shape(32, LANES)],
        [
            (3, 6, *wide),
            (3, 6, *wide),
            (3, 6, *wide),
            (6, *wide),
            (6, *wide),
            (2, 6, *wide),
            (3, 7, *wide),
            (3, 9, *wide),
            (3, 7, *wide),
            (3, 5, *wide),
        ],
        (ids, moments, summed, inner1, outer1, inner2, outer2, p0, p1, p2, e, d, turned),
        12_000_000,
        "basis_second",
    )
    (inbox,) = call(
        inbox_kernel,
        [SM, SM] + [VM] * 4 + [ANY],
        [shape(7, 2 * BLOCK_ROWS, LANES)],
        [],
        (ids, pull_group, kept, *came, basis),
        100_000,
        "inbox",
    )
    gram = lax.all_to_all(gram, "slab", split_axis=0, concat_axis=0, tiled=True)
    correction, element = call(
        last_kernel,
        [SM, VM, VM],
        [shape(3, 3, *plane), shape(1, LANES)],
        [(3, *wide)],
        (ids, gram, basis),
        1_000_000,
        "combine",
    )
    inbox = inbox.reshape(7, BLOCK_ROWS, 2, LANES).transpose(0, 2, 1, 3)
    return (
        correction.reshape(3, 1, DEPTH, FLAT * LANES),
        inbox.reshape(7, 1, 2, BLOCK_ROWS * LANES),
        element[:, :42],
    )


def solution(mesh):
    return jax.shard_map(
        on_device,
        mesh=mesh,
        in_specs=(
            P(None, "rve", "slab", None),
            P("rve", "slab", None),
            P(None, "rve", "slab", None),
            P(None, "rve", "slab", None),
            P("rve", "slab", None),
            P("rve", "slab", None),
            P("rve", "slab", None),
            P(),
            P(),
            P(),
            P(),
        ),
        out_specs=(P(None, "rve", "slab", None), P(None, "rve", "slab", None), P("rve", None)),
        check_vma=False,
    )
```
